32 devices in a mesh: groups: 2 (over y), ensemble: 4 (over z), tensor: 2 (over x), seq: 2 (over core).
Axes of the slice: x: 2, y: 2, z: 4, core: 2. Of those that a mesh axis runs over, the one named last changes fastest.
Arguments:
- pre_act: bfloat16 [768, 4, 8192], P(('groups', 'seq'), 'ensemble', 'tensor'), parts along dimension 0, may hold values from -6 to 6
- weights: bfloat16 [4, 2048, 8192], P('ensemble', 'seq', 'tensor'), may hold values from -0.0625 to 0.0625
- cotangent: bfloat16 [768], P(('groups', 'seq')), parts along dimension 0, may hold values from -24576 to 24576
Outputs:
- weight_grads: bfloat16 [8, 2048, 8192], P(('groups', 'ensemble'), 'seq', 'tensor'), parts along dimension 0
- act_grads: bfloat16 [768, 4, 8192], P(('groups', 'seq'), 'ensemble', 'tensor'), parts along dimension 0
- reward: float32 [768], P(('groups', 'seq')), parts along dimension 0
The draws below stay inside these ranges and needn't reach their ends.
There are 2 independent parts, one for each index of `groups`. The reference program is written for one: setup_inputs(seed, part) draws one part's arguments, and reference() takes and returns one part's arrays. A program takes and returns all parts, laid end to end along the dimension named above; an argument that names none is the same for every part. Nothing has to cross between parts.
All inputs are finite; a program needn't handle non-finite values.
Results may differ from the reference program's by a relative error of at most 0.0076.
Values may be sent and summed in bfloat16 or wider, within the bound.
No kernel may reach another device: no remote copies, remote signals or barrier semaphores. Data moves between devices by JAX's collectives and lax.ppermute only.
A program may use at most 128 MiB of HBM per device.

```python
import jax
import jax.numpy as jnp
from jax import lax

D = 2048
FF = 8192
STEP_DEV = 192
MEMBERS = 4
STEPS = 384
N_SEQ = 2


def steps_of(rng, shape, pieces, least, high):
    factor_of, own = 1.0, jax.random.fold_in(rng, 6)
    for dim, blocks in pieces:
        steps = jnp.exp(jax.random.uniform(jax.random.fold_in(own, dim), (blocks,), jnp.float32, least / len(pieces), high / len(pieces)))
        factor_of = factor_of * jnp.repeat(steps, shape[dim] // blocks).reshape([-1 if axis == dim else 1 for axis in range(len(shape))])
    return factor_of


def noise(rng, shape, width, limit, pieces=(), dtype=jnp.bfloat16):
    array = jax.random.normal(rng, shape, jnp.float32) * width
    if len(pieces) > 0:
        array = steps_of(rng, shape, pieces, -0.22, 0.18) * array
    return jnp.clip(array, min=-limit, max=limit).astype(dtype)


def setup_inputs(seed: int = 0, part: int = 0) -> dict:
    streams_of = jax.random.split(jax.random.key(seed), 4)
    part_keys = jax.random.split(jax.random.fold_in(streams_of[3], part), 4)
    pre_act = noise(part_keys[0], (STEPS, MEMBERS, FF), 1.0, 6.0, ((0, 2), (1, 4), (2, 2)))
    weights = noise(streams_of[1], (MEMBERS, D, FF), FF ** -0.5, 0.0625, ((0, 4), (1, 2), (2, 2)))
    cotangent = noise(part_keys[2], (STEPS,), (MEMBERS * D // 2), 24576.0, ((0, 2),))
    return dict(pre_act=pre_act, weights=weights, cotangent=cotangent)


def reference(pre_act, weights, cotangent):
    activation = pre_act.astype(jnp.float32)
    sigmoid_act = jax.nn.sigmoid(activation)
    hidden = (activation * sigmoid_act).astype(jnp.bfloat16)
    member_hidden = jnp.swapaxes(hidden, 0, 1)

    def predict(pair):
        hid_rows, weight_rows = pair
        return jnp.dot(hid_rows, weight_rows.T, preferred_element_type=jnp.float32)

    predicted = lax.map(predict, (member_hidden, weights))
    member_mean = jnp.sum(predicted, axis=0) / MEMBERS
    squares = jnp.sum(predicted * predicted, axis=(0, 2))
    reward = (squares / MEMBERS - jnp.sum(member_mean * member_mean, axis=1)) / D
    weighting = cotangent.astype(jnp.float32) * (2.0 / (MEMBERS * D))

    def backward(triple):
        hid_rows, weight_rows, pred_rows = triple
        grad_pred = (weighting[:, None] * (pred_rows - member_mean)).astype(jnp.bfloat16)
        accumulated = jnp.zeros((D, FF), jnp.float32)
        for block_index in range(N_SEQ):
            lower = block_index * STEP_DEV
            block_term = jnp.dot(grad_pred[lower:lower + STEP_DEV].T, hid_rows[lower:lower + STEP_DEV], preferred_element_type=jnp.float32).astype(jnp.bfloat16)
            block_term = lax.optimization_barrier(block_term)
            accumulated = accumulated + block_term.astype(jnp.float32)
        grad_hidden = jnp.dot(grad_pred, weight_rows, preferred_element_type=jnp.float32)
        return accumulated.astype(jnp.bfloat16), grad_hidden

    weight_grads, grad_hidden = lax.map(backward, (member_hidden, weights, predicted))
    slope = sigmoid_act * (1.0 + activation * (1.0 - sigmoid_act))
    act_grads = (jnp.swapaxes(grad_hidden, 0, 1) * slope).astype(jnp.bfloat16)
    return weight_grads, act_grads, reward
```

```python
import jax
import jax.numpy as jnp
from jax import lax
from jax.sharding import PartitionSpec as P

F32, BF16 = jnp.float32, jnp.bfloat16
NT = (((1,), (1,)), ((), ()))
TN = (((0,), (0,)), ((), ()))
PIECES = 2


def swap(value, axis, distance):
    size = lax.axis_size(axis)
    return lax.ppermute(value, axis, [(i, i ^ distance) for i in range(size)])


def shares(size):
    return [1 << bit for bit in range(size.bit_length() - 1)]


def silu(value):
    wide = value.astype(F32)
    return (wide * jax.nn.sigmoid(wide)).astype(BF16)


def project(hidden, weights, start, width):
    rows = lax.dynamic_slice_in_dim(weights, start, width, 0)
    return lax.dot_general(hidden, rows, NT, preferred_element_type=F32)


def own_prediction(hidden, weights, start, width):
    place = lax.axis_index("tensor")
    offset = start
    kept = None
    for distance in reversed(shares(lax.axis_size("tensor"))):
        width //= 2
        high = (place // distance) % 2
        if kept is None:
            sent = project(hidden, weights, offset + (1 - high) * width, width)
            mine = project(hidden, weights, offset + high * width, width)
        else:
            sent = lax.dynamic_slice_in_dim(kept, (1 - high) * width, width, 1)
            mine = lax.dynamic_slice_in_dim(kept, high * width, width, 1)
        offset = offset + high * width
        kept = mine + swap(sent.astype(BF16), "tensor", distance).astype(F32)
    return kept


def member_mean_of(predicted):
    total = predicted
    for distance in shares(lax.axis_size("ensemble")):
        total = total + swap(total.astype(BF16), "ensemble", distance).astype(F32)
    return total / lax.axis_size("ensemble")


def all_features(share):
    place = lax.axis_index("tensor")
    for distance in shares(lax.axis_size("tensor")):
        other = swap(share, "tensor", distance)
        high = (place // distance) % 2
        first = jnp.where(high == 0, share, other)
        second = jnp.where(high == 0, other, share)
        share = jnp.concatenate([first, second], axis=1)
    return share


def body(pre_act, weights, cotangent):
    pre_act, weights = pre_act[:, 0, :], weights[0]
    steps, hidden_units = pre_act.shape
    features = weights.shape[0]
    members = lax.axis_size("ensemble")
    model_width = features * lax.axis_size("seq")
    factor = 2.0 / (members * model_width)

    pre_other = swap(pre_act, "seq", 1)
    cot_other = swap(cotangent, "seq", 1)
    hidden = (silu(pre_act), silu(pre_other))
    weighting = [c.astype(F32)[:, None] * factor for c in (cotangent, cot_other)]
    width = features // PIECES
    order = [(0, 0), (1, 0), (1, 1), (0, 1)]
    grads, spreads = {}, {}
    for side, piece in order:
        predicted = own_prediction(hidden[side], weights, piece * width, width)
        gap = predicted - member_mean_of(predicted)
        spreads[side, piece] = jnp.sum(gap * gap, axis=1)
        grads[side, piece] = all_features((weighting[side] * gap).astype(BF16))
    weight_grads, grad_hidden = [], [None, None]
    for piece in range(PIECES):
        terms = [
            lax.dot_general(grads[s, piece], hidden[s], TN, preferred_element_type=F32)
            for s in range(2)
        ]
        weight_grads.append((terms[0] + terms[1]).astype(BF16))
        rows = weights[piece * width : (piece + 1) * width]
        for side in range(2):
            term = jnp.dot(grads[side, piece], rows, preferred_element_type=F32)
            before = grad_hidden[side]
            grad_hidden[side] = term if before is None else before + term
    arrived = swap(grad_hidden[1].astype(BF16), "seq", 1).astype(F32)
    activation = pre_act.astype(F32)
    sigmoid_act = jax.nn.sigmoid(activation)
    slope = sigmoid_act * (1.0 + activation * (1.0 - sigmoid_act))
    act_grads = ((grad_hidden[0] + arrived) * slope).astype(BF16)
    both = jnp.stack([sum(spreads[s, p] for p in range(PIECES)) for s in range(2)])
    for axis in ("ensemble", "tensor"):
        for distance in shares(lax.axis_size(axis)):
            both = both + swap(both, axis, distance)
    spread = both[0] + swap(both[1], "seq", 1)
    reward = spread / (members * model_width)
    return (jnp.concatenate(weight_grads)[None], act_grads[:, None, :], reward)


def solution(mesh):
    placed = (
        P(("groups", "seq"), "ensemble", "tensor"),
        P("ensemble", "seq", "tensor"),
        P(("groups", "seq")),
    )
    return jax.shard_map(
        body,
        mesh=mesh,
        in_specs=placed,
        out_specs=(
            P(("groups", "ensemble"), "seq", "tensor"),
            P(("groups", "seq"), "ensemble", "tensor"),
            P(("groups", "seq")),
        ),
        check_vma=False,
    )
```

```python
import functools

import jax
import jax.numpy as jnp
from jax import lax
from jax.experimental import pallas as pl
from jax.experimental.pallas import tpu as pltpu
from jax.sharding import PartitionSpec as P

F32, BF16 = jnp.float32, jnp.bfloat16
NT = (((1,), (1,)), ((), ()))
TN = (((0,), (0,)), ((), ()))
PIECES = 2
SCALE = 0.2
VMEM_LIMIT = 16 * 2**20


def swap(value, axis, distance):
    size = lax.axis_size(axis)
    return lax.ppermute(value, axis, [(i, i ^ distance) for i in range(size)])


def shares(size):
    return [1 << bit for bit in range(size.bit_length() - 1)]


def sigmoid(wide):
    return jax.nn.sigmoid(wide)


def silu(value):
    wide = value.astype(F32)
    return (wide * sigmoid(wide)).astype(BF16)


VMEM = pl.BlockSpec(memory_space=pltpu.VMEM)
HBM = pl.BlockSpec(memory_space=pltpu.HBM)


def in_vmem(shape, dtype):
    return pltpu.VMEM(shape, dtype)


def in_hbm(shape, dtype):
    return pltpu.HBM(shape, dtype)


def call(kernel, out_shape, in_specs, scratch=(), aliases=None, work=0.1, name=None):
    outs = out_shape if isinstance(out_shape, list) else [out_shape]
    out_specs = [pl.BlockSpec(memory_space=out.memory_space) for out in outs]
    run = pl.pallas_call(
        kernel,
        out_shape=outs,
        in_specs=in_specs,
        out_specs=out_specs,
        scratch_shapes=list(scratch),
        input_output_aliases=aliases or {},
        compiler_params=pltpu.CompilerParams(vmem_limit_bytes=VMEM_LIMIT),
        cost_estimate=pl.CostEstimate(
            flops=int(work * SCALE * 1e9), bytes_accessed=1, transcendentals=0
        ),
        name=name,
    )

    def placed(*operands):
        operands = [
            pltpu.with_memory_space_constraint(value, spec.memory_space)
            for value, spec in zip(operands, in_specs)
        ]
        result = run(*operands)
        return result if isinstance(out_shape, list) else result[0]

    return placed


def cuts(whole, parts):
    return [pl.ds(at * (whole // parts), whole // parts) for at in range(parts)]


def number(numbers_ref, at, step):
    return pl.multiple_of(numbers_ref[at, 0], step)


def start_copy(source, target, sem):
    copy = pltpu.make_async_copy(source, target, sem)
    copy.start()
    return copy


def split(rows, width):
    count, steps = rows.shape
    parts = []
    for _ in range(3):
        part = rows.astype(BF16).astype(F32)
        parts.append(part)
        rows = rows - part
    parts.append(jnp.zeros((16 - 3 * count, steps), F32))
    out = jnp.concatenate(parts, axis=0)
    if width > steps:
        out = jnp.concatenate([out, jnp.zeros((16, width - steps), F32)], axis=1)
    return out.astype(BF16)


def joined(parts, steps):
    wide = parts[:, :steps].astype(F32)
    return wide[:2] + wide[2:4] + wide[4:6]


def load_first(source, weights, starts, half):
    steps, units = source.shape
    spans = 4
    width = units // spans

    def kernel(starts_ref, source_ref, weights_ref, sent_ref, hidden_ref, held, pre, total, sems):
        rows = pl.ds(number(starts_ref, 0, half), half)

        def copies(at):
            span = pl.ds(pl.multiple_of(at * width, width), width)
            return span, (
                pltpu.make_async_copy(source_ref.at[:, span], pre.at[:, span], sems.at[0, at]),
                pltpu.make_async_copy(
                    weights_ref.at[rows, span], held.at[:, span], sems.at[1, at]
                ),
            )

        def start(at):
            for copy in copies(at)[1]:
                copy.start()

        start(0)
        start(1)
        total[...] = jnp.zeros_like(total)

        def step(at, carry):
            @pl.when(at + 2 < spans)
            def _():
                start(at + 2)

            span, pair = copies(at)
            for copy in pair:
                copy.wait()
            hidden = silu(pre[:, span])
            hidden_ref[:, span] = hidden
            total[...] += lax.dot_general(
                hidden, held[:, span], NT, preferred_element_type=F32
            )
            return carry

        lax.fori_loop(0, spans, step, 0)
        sent_ref[...] = total[...].astype(BF16)

    return call(
        kernel,
        [
            in_vmem((steps, half), BF16),
            in_vmem((steps, units), BF16),
            in_vmem((half, units), BF16),
            in_vmem((steps, units), BF16),
        ],
        [VMEM, HBM, HBM],
        [pltpu.VMEM((steps, half), F32), pltpu.SemaphoreType.DMA((2, spans))],
        work=3.2, name="load_first",
    )(starts, source, weights)


def load_second(source, weights, starts, held, own_sent):
    steps, units = source.shape
    half = held.shape[0]

    def kernel(
        starts_ref, source_ref, weights_ref, held_ref, own_ref, out_ref, hidden_ref, block, sem
    ):
        first = number(starts_ref, 1, half)
        copy = start_copy(weights_ref.at[pl.ds(first, half), :], block, sem)

        @pl.when(first >= 0)
        def _():
            out_ref[pl.ds(0, steps), :] = own_ref[...]
            total = None
            for span in cuts(units, 4):
                hidden = silu(source_ref[:, span])
                hidden_ref[:, span] = hidden
                term = lax.dot_general(hidden, held_ref[:, span], NT, preferred_element_type=F32)
                total = term if total is None else total + term
            out_ref[pl.ds(steps, steps), :] = total.astype(BF16)

        copy.wait()

    return call(
        kernel,
        [
            in_vmem((2 * steps, half), BF16),
            in_vmem((steps, units), BF16),
            in_vmem((half, units), BF16),
        ],
        [VMEM, VMEM, HBM, VMEM, VMEM],
        [pltpu.SemaphoreType.DMA],
        work=1.6, name="load_second",
    )(starts, source, weights, held, own_sent)


def project(hidden, rows, out_type, weights, starts, following):
    steps, units = hidden[0].shape
    half = rows.shape[0]
    more = following is not None

    def products(hidden_refs, rows_ref, out_ref):
        for at, hidden_ref in enumerate(hidden_refs):
            total = lax.dot_general(
                hidden_ref[...], rows_ref[...], NT, preferred_element_type=F32
            )
            out_ref[pl.ds(at * steps, steps), :] = total.astype(out_type)

    def kernel(first, second, rows_ref, out_ref):
        products((first, second), rows_ref, out_ref)

    def loading(starts_ref, weights_ref, first, second, rows_ref, out_ref, block, sem):
        start = number(starts_ref, following, half)
        copy = start_copy(weights_ref.at[pl.ds(start, half), :], block, sem)

        @pl.when(start >= 0)
        def _():
            products((first, second), rows_ref, out_ref)

        copy.wait()

    out_shape = in_vmem((2 * steps, half), out_type)
    if not more:
        return [call(kernel, out_shape, [VMEM] * 3, work=1.6, name="project")(*hidden, rows)]
    return call(
        loading,
        [out_shape, in_vmem((half, units), BF16)],
        [VMEM, HBM, VMEM, VMEM, VMEM],
        [pltpu.SemaphoreType.DMA],
        work=1.6, name="project",
    )(starts, weights, *hidden, rows)


def lane_sums(value):
    width = value.shape[1]
    if width % 128 == 0:
        squares = value * value
        squares = sum(squares[:, at : at + 128] for at in range(0, width, 128))
        return jnp.sum(squares.T, axis=0, keepdims=True)
    ones = jnp.ones((8, value.shape[1]), F32)
    sums = lax.dot_general(
        ones, value * value, NT, precision=lax.Precision.HIGHEST, preferred_element_type=F32
    )
    return sums[:1]


def half_of(place, steps):
    return pl.ds(pl.multiple_of(place * steps, steps), steps)


def predicted_of(kept, arriving, starts, squares, packed):
    steps, width = kept.shape[0] // 2, kept.shape[1]

    def kernel(starts_ref, kept_ref, arriving_ref, *refs):
        sent_ref, total_ref, squares_ref = refs[-3:]
        rows = []
        for at in range(2):
            part = pl.ds(at * steps, steps)
            total = kept_ref[part, :] + arriving_ref[part, :].astype(F32)
            total_ref[part, :] = total
            rows.append(lane_sums(total))
        sent_ref[pl.ds(0, steps), :] = total_ref[half_of(1 - starts_ref[7, 0], steps), :].astype(BF16)
        both = jnp.concatenate(rows, axis=0)
        if squares is not None:
            both += refs[0][...]
        squares_ref[...] = both
        if packed:
            sent_ref[pl.ds(steps, 16), :] = split(both, width)

    shapes = [
        in_vmem((steps + 16 * packed, width), BF16),
        in_vmem((2 * steps, width), F32),
        in_vmem((2, steps), F32),
    ]
    more = [] if squares is None else [squares]
    return call(kernel, shapes, [VMEM] + [VMEM] * (2 + len(more)), work=0.2, name="predicted")(
        starts, kept, arriving, *more
    )


def sum_of(total, arriving, starts, squares, packed, out_packed):
    steps, width = arriving.shape[0] - 16 * packed, arriving.shape[1]

    def kernel(starts_ref, total_ref, arriving_ref, squares_ref, sent_ref, out_ref, both_ref):
        held = total_ref[half_of(starts_ref[7, 0], steps), :] if total.shape[0] > steps else total_ref[...]
        out = held + arriving_ref[pl.ds(0, steps), :].astype(F32)
        sent_ref[pl.ds(0, steps), :] = out.astype(BF16)
        out_ref[...] = out
        both = squares_ref[...]
        if packed:
            both += joined(arriving_ref[pl.ds(steps, 16), :], both.shape[1])
        both_ref[...] = both
        if out_packed:
            sent_ref[pl.ds(steps, 16), :] = split(both, width)

    shapes = [
        in_vmem((steps + 16 * out_packed, width), BF16),
        in_vmem((steps, width), F32),
        in_vmem(squares.shape, F32),
    ]
    return call(kernel, shapes, [VMEM, VMEM, VMEM, VMEM], name="sum_of")(
        starts, total, arriving, squares
    )


def gradient_of(total, arriving, predicted, starts, cotangents, before, members, factor, packed):
    steps, width = total.shape
    last, previous = before

    def kernel(starts_ref, total_ref, arriving_ref, predicted_ref, own, other, *refs):
        grad_ref, sums_ref, mean_ref = refs[-3:]
        mean_ref[half_of(starts_ref[7, 0], steps), :] = total_ref[...] / members
        mean_ref[half_of(1 - starts_ref[7, 0], steps), :] = arriving_ref[...].astype(F32) / members
        rows = []
        for at, cotangent_ref in enumerate((own, other)):
            part = pl.ds(at * steps, steps)
            mean = mean_ref[part, :]
            weighting = cotangent_ref[:, :1].astype(F32) * factor
            grad_ref[part, :] = (weighting * (predicted_ref[part, :] - mean)).astype(BF16)
            rows.append(lane_sums(mean))
        both = jnp.concatenate(rows, axis=0)
        if previous is not None:
            both += refs[0][...]
        if last is not None:
            both = refs[-4][...] / members - both
        sums_ref[...] = both
        if packed:
            grad_ref[pl.ds(2 * steps, 16), :] = split(both, width)

    shapes = [in_vmem((2 * steps + 16 * packed, width), BF16), in_vmem((2, steps), F32)]
    more = [value for value in (previous, last) if value is not None]
    return call(
        kernel,
        shapes,
        [VMEM] + [VMEM] * (5 + len(more)),
        [pltpu.VMEM((2 * steps, width), F32)],
        work=0.3, name="gradient",
    )(starts, total, arriving, predicted, *cotangents, *more)


def plus(first, second):
    def kernel(first_ref, second_ref, out_ref):
        out_ref[...] = first_ref[...] + second_ref[...]

    return call(kernel, in_vmem(first.shape, F32), [VMEM, VMEM], name="plus")(first, second)


def leave_to_other(grad, rows, before, spread, arriving_spread, steps):
    units = rows.shape[1]
    packed = arriving_spread.shape[0] > 2

    def kernel(grad_ref, rows_ref, before_ref, spread_ref, arriving_ref, out_ref, sum_ref):
        for span in cuts(units, 4):
            term = jnp.dot(
                grad_ref[pl.ds(steps, steps), :], rows_ref[:, span], preferred_element_type=F32
            )
            out_ref[pl.ds(0, steps), span] = (before_ref[:, span] + term).astype(BF16)
        if packed:
            both = spread_ref[...] + joined(arriving_ref[pl.ds(2 * steps, 16), :], steps)
        else:
            both = spread_ref[...] + arriving_ref[...]
        sum_ref[...] = both
        out_ref[pl.ds(steps, 16), :] = split(both, units)

    shapes = [in_vmem((steps + 16, units), BF16), in_vmem((2, steps), F32)]
    return call(kernel, shapes, [VMEM] * 5, work=0.6, name="leave_to_other")(
        grad, rows, before, spread, arriving_spread
    )


def block_rows(grad, hidden, steps, rows):
    total = lax.dot_general(
        grad[pl.ds(0, steps), rows], hidden[0][...], TN, preferred_element_type=F32
    )
    total += lax.dot_general(
        grad[pl.ds(steps, steps), rows], hidden[1][...], TN, preferred_element_type=F32
    )
    return total.astype(BF16)


def write_rows(start, grad, hidden, steps, made, out_ref, sems):
    half = made.shape[0]
    copies = []
    for at, rows in enumerate(cuts(half, 2)):
        made[rows, :] = block_rows(grad, hidden, steps, rows)
        to = pl.ds(pl.multiple_of(start + rows.start, rows.size), rows.size)
        copies.append(start_copy(made.at[rows, :], out_ref.at[to, :], sems.at[at]))
    return copies


def weight_rows(grads, hidden, starts, blocks, features, started=None, back=()):
    half, (steps, units) = grads[0].shape[1], hidden[0].shape
    more = [] if started is None else [started]
    operands, plan = [], []
    for part, pairs, before in back:
        plan.append((part, len(pairs), before is not None))
        operands += [value for pair in pairs for value in pair]
        operands += [] if before is None else [before]

    def kernel(starts_ref, *refs):
        refs = list(refs)
        take = lambda count: [refs.pop(0) for _ in range(count)]
        grad_refs, hidden_refs, operand_refs = take(len(grads)), take(2), take(len(operands))
        take(len(more))
        (out_ref,), sum_refs, (made, sems) = take(1), take(len(back)), take(2)
        copies = []
        for at, (block, grad) in enumerate(zip(blocks, grad_refs)):
            copies += write_rows(
                starts_ref[block, 0],
                grad,
                hidden_refs,
                steps,
                made.at[at],
                out_ref,
                sems.at[at],
            )
        for (part, count, added), sum_ref in zip(plan, sum_refs):
            pairs = [(operand_refs.pop(0), operand_refs.pop(0)) for _ in range(count)]
            before_ref = operand_refs.pop(0) if added else None
            for span in cuts(units, 4):
                out = before_ref[:, span] if added else None
                for grad, rows in pairs:
                    term = jnp.dot(
                        grad[pl.ds(part * steps, steps), :],
                        rows[:, span],
                        preferred_element_type=F32,
                    )
                    out = term if out is None else out + term
                sum_ref[:, span] = out
        for copy in copies:
            copy.wait()

    result = call(
        kernel,
        [in_hbm((features, units), BF16)] + [in_vmem((steps, units), F32)] * len(back),
        [VMEM] * (3 + len(grads) + len(operands)) + [HBM] * len(more),
        [
            pltpu.VMEM((len(grads), half, units), BF16),
            pltpu.SemaphoreType.DMA((len(grads), 2)),
        ],
        aliases={3 + len(grads) + len(operands): 0} if more else None,
        work=2 * len(grads) + len(back), name="weight_rows",
    )(starts, *grads, *hidden, *operands, *more)
    return result


def last_grads(before, arrived, pre_act, spread, model_width):
    steps, units = before.shape
    lanes = -(-steps // 128) * 128

    def kernel(before_ref, arrived_ref, pre, spread_ref, act_ref, reward_ref, act, reward, sems):
        others = joined(arrived_ref[pl.ds(steps, 16), pl.ds(0, lanes)], steps)
        reward[...] = (spread_ref[...][:1] + others[1:]) / model_width
        copies = [start_copy(reward, reward_ref, sems.at[4])]
        for at, span in enumerate(cuts(units, 4)):
            wide = pre[:, span].astype(F32)
            gate = sigmoid(wide)
            slope = gate * (1.0 + wide * (1.0 - gate))
            total = before_ref[:, span] + arrived_ref[pl.ds(0, steps), span].astype(F32)
            act[:, span] = (total * slope).astype(BF16)
            copies.append(start_copy(act.at[:, span], act_ref.at[:, span], sems.at[at]))
        for copy in copies:
            copy.wait()

    return call(
        kernel,
        [in_hbm((steps, units), BF16), in_hbm((1, steps), F32)],
        [VMEM] * 4,
        [
            pltpu.VMEM((steps, units), BF16),
            pltpu.VMEM((1, steps), F32),
            pltpu.SemaphoreType.DMA((5,)),
        ],
        work=1.9, name="last_grads",
    )(before, arrived, pre_act, spread)


class Order:
    def __init__(self):
        self.last = None

    def __call__(self, step, *values):
        if self.last is not None:
            values, _ = lax.optimization_barrier((values, self.last))
        result = step(*values)
        self.last = jax.tree.leaves(result)[0]
        return result


class Piece:
    def __init__(self, order, starts, last, previous):
        self.order, self.starts = order, starts
        self.last, self.previous = last, previous
        self.tensor = lax.axis_index("tensor")

    def leave(self, sent):
        self.arriving = swap(sent, "tensor", shares(lax.axis_size("tensor"))[-1])

    def scatter_rest(self):
        def add(total, arriving):
            return total + arriving.astype(F32)

        for distance in reversed(shares(lax.axis_size("tensor"))[:-1]):
            half = self.total.shape[1] // 2
            high = (self.tensor // distance) % 2
            total = self.order(add, self.total, self.arriving)
            sent = lax.dynamic_slice_in_dim(total, (1 - high) * half, half, 1)
            self.total = lax.dynamic_slice_in_dim(total, high * half, half, 1)
            self.arriving = swap(sent.astype(BF16), "tensor", distance)

    def predict(self):
        steps, width = self.total.shape[0] // 2, self.total.shape[1]
        self.packed = self.last and width >= steps
        before = None if self.previous is None else self.previous.squares
        sent, self.predicted, self.squares = self.order(
            lambda kept, arriving: predicted_of(kept, arriving, self.starts, before, self.packed),
            self.total,
            self.arriving,
        )
        self.sum = self.predicted
        near, *self.far = shares(lax.axis_size("ensemble"))
        self.arriving = swap(sent, "ensemble", near)
        self.exchange_squares(near)

    def exchange_squares(self, distance):
        self.squares_arriving = None
        if self.last and not self.packed:
            self.squares_arriving = swap(self.squares, "ensemble", distance)

    def ensemble_steps(self):
        packed = self.packed
        for distance in self.far + [None]:
            out_packed = self.packed and distance is not None
            sent, self.sum, squares = self.order(
                lambda total, arriving: sum_of(
                    total, arriving, self.starts, self.squares, packed, out_packed
                ),
                self.sum,
                self.arriving,
            )
            if self.squares_arriving is not None:
                squares = self.order(plus, squares, self.squares_arriving)
            self.squares = squares
            if distance is not None:
                self.arriving = swap(sent, "ensemble", distance)
                self.exchange_squares(distance)
                yield
            else:
                self.arriving = swap(sent, "ensemble", 1)

    def gradient(self, cotangents, members, factor):
        def join(share, other, distance):
            high = (self.tensor // distance) % 2
            first = jnp.where(high == 0, share, other)
            second = jnp.where(high == 0, other, share)
            return jnp.concatenate([first, second], axis=1)

        *near, far = shares(lax.axis_size("tensor"))
        packed = self.last and not near and self.sum.shape[1] >= self.sum.shape[0]
        before = (
            self.squares if self.last else None,
            None if self.previous is None else self.previous.sums,
        )
        self.share, self.sums = self.order(
            lambda total, arriving: gradient_of(
                total,
                arriving,
                self.predicted,
                self.starts,
                cotangents,
                before,
                members,
                factor,
                packed,
            ),
            self.sum,
            self.arriving,
        )
        for distance in near:
            other = swap(self.share, "tensor", distance)
            self.share = self.order(functools.partial(join, distance=distance), self.share, other)
        self.other = swap(self.share, "tensor", far)
        if self.last and not packed:
            for distance in near:
                self.sums = self.order(plus, self.sums, swap(self.sums, "tensor", distance))
            self.other_sums = swap(self.sums, "tensor", far)
        else:
            self.other_sums = self.other


def body(pre_act, weights, cotangent):
    pre_act, weights = pre_act[:, 0, :], weights[0]
    steps, features = pre_act.shape[0], weights.shape[0]
    members = lax.axis_size("ensemble")
    model_width = features * lax.axis_size("seq")
    factor = 2.0 / (members * model_width)
    half = features // (2 * PIECES)
    far = shares(lax.axis_size("tensor"))[-1]
    high = (lax.axis_index("tensor") // far) % 2
    starts = []
    for piece in range(PIECES):
        starts += [(2 * piece + 1 - high) * half, (2 * piece + high) * half]
    assert len(starts) < 8
    starts += [0] * (7 - len(starts)) + [lax.axis_index("ensemble") % 2]
    starts = jnp.broadcast_to(jnp.stack(starts).astype(jnp.int32)[:, None], (8, 128))

    pre_other = swap(pre_act, "seq", 1)
    pre_act, starts = lax.optimization_barrier((pre_act, starts))
    order = Order()
    pieces = []
    for at in range(PIECES):
        previous = pieces[-1] if pieces else None
        pieces.append(Piece(order, starts, at == PIECES - 1, previous))
    blocks = [None] * (2 * PIECES)
    own_sent, hidden, blocks[0], pre_act = order(
        lambda p: load_first(p, weights, starts, half), pre_act
    )
    sent, hidden_other, blocks[1] = order(
        lambda p, s: load_second(p, weights, starts, blocks[0], s), pre_other, own_sent
    )
    both = [hidden, hidden_other]
    pieces[0].leave(sent)
    for at in range(1, 2 * PIECES):
        out_type = F32 if at % 2 else BF16
        out = order(
            lambda rows: project(
                both, rows, out_type, weights, starts, at + 1 if at + 1 < 2 * PIECES else None
            ),
            blocks[at],
        )
        if at + 1 < 2 * PIECES:
            blocks[at + 1] = out[1]
        if at % 2:
            pieces[at // 2].total = out[0]
        else:
            pieces[at // 2].leave(out[0])

    wide = order(lambda c: jnp.broadcast_to(c[:, None], (steps, 128)), cotangent)
    cotangents = [wide, swap(wide, "seq", 1)]
    running = []
    for piece in pieces:
        piece.scatter_rest()
        piece.predict()
        running.append(piece.ensemble_steps())
        for other in running[:-1]:
            next(other, None)
    a, b = pieces
    for other in running:
        next(other, None)
    next(running[0], None)
    a.gradient(cotangents, members, factor)
    (weight_grads,) = order(
        lambda g: weight_rows([g], both, starts, [1], features), a.share
    )
    for other in running:
        for _ in other:
            pass
    b.gradient(cotangents, members, factor)

    def middle(a_share, a_other, b_share, weight_grads):
        pairs = [(a_share, blocks[1]), (a_other, blocks[0]), (b_share, blocks[3])]
        back = [(1, pairs, None), (0, pairs, None)]
        return weight_rows(
            [b_share, a_other], both, starts, [3, 0], features, weight_grads, back
        )

    weight_grads, before_other, before = order(middle, a.share, a.other, b.share, weight_grads)
    leaving, spread = order(
        lambda g, s: leave_to_other(g, blocks[2], before_other, b.sums, s, steps),
        b.other,
        b.other_sums,
    )
    arrived = swap(leaving, "seq", 1)
    weight_grads, before = order(
        lambda g, s: weight_rows(
            [g], both, starts, [2], features, s, [(0, [(g, blocks[2])], before)]
        ),
        b.other,
        weight_grads,
    )
    act_grads, reward = order(
        lambda g, s: last_grads(g, s, pre_act, spread, model_width), before, arrived
    )
    return (weight_grads[None], act_grads[:, None, :], reward[0])


def solution(mesh):
    placed = (
        P(("groups", "seq"), "ensemble", "tensor"),
        P("ensemble", "seq", "tensor"),
        P(("groups", "seq")),
    )
    return jax.shard_map(
        body,
        mesh=mesh,
        in_specs=placed,
        out_specs=(
            P(("groups", "ensemble"), "seq", "tensor"),
            P(("groups", "seq"), "ensemble", "tensor"),
            P(("groups", "seq")),
        ),
        check_vma=False,
    )
```

```python
import functools

import jax
import jax.numpy as jnp
from jax import lax
from jax.experimental import pallas as pl
from jax.experimental.pallas import tpu as pltpu
from jax.sharding import PartitionSpec as P

F32, BF16 = jnp.float32, jnp.bfloat16
NT = (((1,), (1,)), ((), ()))
TN = (((0,), (0,)), ((), ()))
PIECES = 2
WORK = 0.6
VMEM_LIMIT = 16 * 2**20


def swap(value, axis, distance):
    size = lax.axis_size(axis)
    return lax.ppermute(value, axis, [(i, i ^ distance) for i in range(size)])


def shares(size):
    return [1 << bit for bit in range(size.bit_length() - 1)]


def sigmoid(wide):
    return jax.nn.sigmoid(wide)


def silu(value):
    wide = value.astype(F32)
    return (wide * sigmoid(wide)).astype(BF16)


VMEM = pl.BlockSpec(memory_space=pltpu.VMEM)
HBM = pl.BlockSpec(memory_space=pltpu.HBM)


def in_vmem(shape, dtype):
    return pltpu.VMEM(shape, dtype)


def in_hbm(shape, dtype):
    return pltpu.HBM(shape, dtype)


def call(kernel, out_shape, in_specs, scratch=(), aliases=None, name=None):
    outs = out_shape if isinstance(out_shape, list) else [out_shape]
    out_specs = [pl.BlockSpec(memory_space=out.memory_space) for out in outs]
    run = pl.pallas_call(
        kernel,
        out_shape=outs,
        in_specs=in_specs,
        out_specs=out_specs,
        scratch_shapes=list(scratch),
        input_output_aliases=aliases or {},
        compiler_params=pltpu.CompilerParams(vmem_limit_bytes=VMEM_LIMIT),
        cost_estimate=pl.CostEstimate(
            flops=int(WORK * 1e9), bytes_accessed=1, transcendentals=0
        ),
        name=name,
    )

    def placed(*operands):
        operands = [
            pltpu.with_memory_space_constraint(value, spec.memory_space)
            for value, spec in zip(operands, in_specs)
        ]
        result = run(*operands)
        return result if isinstance(out_shape, list) else result[0]

    return placed


def cuts(whole, parts):
    return [pl.ds(at * (whole // parts), whole // parts) for at in range(parts)]


def number(numbers_ref, at, step):
    return pl.multiple_of(numbers_ref[at, 0], step)


def start_copy(source, target, sem):
    copy = pltpu.make_async_copy(source, target, sem)
    copy.start()
    return copy


def split(rows, width):
    count, steps = rows.shape
    parts = []
    for _ in range(3):
        part = rows.astype(BF16).astype(F32)
        parts.append(part)
        rows = rows - part
    parts.append(jnp.zeros((16 - 3 * count, steps), F32))
    out = jnp.concatenate(parts, axis=0)
    if width > steps:
        out = jnp.concatenate([out, jnp.zeros((16, width - steps), F32)], axis=1)
    return out.astype(BF16)


def joined(parts, steps):
    wide = parts[:, :steps].astype(F32)
    return wide[:2] + wide[2:4] + wide[4:6]


def load_first(source, weights, starts, half):
    steps, units = source.shape
    spans = 4
    width = units // spans

    def kernel(starts_ref, source_ref, weights_ref, sent_ref, hidden_ref, held, pre, total, sems):
        rows = pl.ds(number(starts_ref, 0, half), half)

        def copies(at):
            span = pl.ds(pl.multiple_of(at * width, width), width)
            return span, (
                pltpu.make_async_copy(source_ref.at[:, span], pre.at[:, span], sems.at[0, at]),
                pltpu.make_async_copy(
                    weights_ref.at[rows, span], held.at[:, span], sems.at[1, at]
                ),
            )

        def start(at):
            for copy in copies(at)[1]:
                copy.start()

        start(0)
        start(1)
        total[...] = jnp.zeros_like(total)

        def step(at, carry):
            @pl.when(at + 2 < spans)
            def _():
                start(at + 2)

            span, pair = copies(at)
            for copy in pair:
                copy.wait()
            hidden = silu(pre[:, span])
            hidden_ref[:, span] = hidden
            total[...] += lax.dot_general(
                hidden, held[:, span], NT, preferred_element_type=F32
            )
            return carry

        lax.fori_loop(0, spans, step, 0)
        sent_ref[...] = total[...].astype(BF16)

    return call(
        kernel,
        [
            in_vmem((steps, half), BF16),
            in_vmem((steps, units), BF16),
            in_vmem((half, units), BF16),
            in_vmem((steps, units), BF16),
        ],
        [VMEM, HBM, HBM],
        [pltpu.VMEM((steps, half), F32), pltpu.SemaphoreType.DMA((2, spans))],
        name="load_first",
    )(starts, source, weights)


def load_second(source, weights, starts, held, following):
    steps, units = source.shape
    half = held.shape[0]

    def kernel(starts_ref, source_ref, weights_ref, held_ref, out_ref, hidden_ref, block, sem):
        first = number(starts_ref, following, half)
        copy = start_copy(weights_ref.at[pl.ds(first, half), :], block, sem)

        @pl.when(first >= 0)
        def _():
            total = None
            for span in cuts(units, 4):
                hidden = silu(source_ref[:, span])
                hidden_ref[:, span] = hidden
                term = lax.dot_general(hidden, held_ref[:, span], NT, preferred_element_type=F32)
                total = term if total is None else total + term
            out_ref[...] = total.astype(BF16)

        copy.wait()

    return call(
        kernel,
        [
            in_vmem((steps, half), BF16),
            in_vmem((steps, units), BF16),
            in_vmem((half, units), BF16),
        ],
        [VMEM, VMEM, HBM, VMEM],
        [pltpu.SemaphoreType.DMA],
        name="load_second",
    )(starts, source, weights, held)


def project(hidden, rows, out_type, weights, starts, following):
    steps, units = hidden[0].shape
    half = rows.shape[0]
    more = following is not None

    def products(hidden_refs, rows_ref, out_ref):
        for at, hidden_ref in enumerate(hidden_refs):
            total = lax.dot_general(
                hidden_ref[...], rows_ref[...], NT, preferred_element_type=F32
            )
            out_ref[pl.ds(at * steps, steps), :] = total.astype(out_type)

    def kernel(first, second, rows_ref, out_ref):
        products((first, second), rows_ref, out_ref)

    def loading(starts_ref, weights_ref, first, second, rows_ref, out_ref, block, sem):
        start = number(starts_ref, following, half)
        copy = start_copy(weights_ref.at[pl.ds(start, half), :], block, sem)

        @pl.when(start >= 0)
        def _():
            products((first, second), rows_ref, out_ref)

        copy.wait()

    out_shape = in_vmem((2 * steps, half), out_type)
    if not more:
        return [call(kernel, out_shape, [VMEM] * 3, name="project")(*hidden, rows)]
    return call(
        loading,
        [out_shape, in_vmem((half, units), BF16)],
        [VMEM, HBM, VMEM, VMEM, VMEM],
        [pltpu.SemaphoreType.DMA],
        name="project",
    )(starts, weights, *hidden, rows)


def lane_sums(value):
    width = value.shape[1]
    if width % 128 == 0:
        squares = value * value
        squares = sum(squares[:, at : at + 128] for at in range(0, width, 128))
        return jnp.sum(squares.T, axis=0, keepdims=True)
    ones = jnp.ones((8, value.shape[1]), F32)
    sums = lax.dot_general(
        ones, value * value, NT, precision=lax.Precision.HIGHEST, preferred_element_type=F32
    )
    return sums[:1]


def half_of(place, steps):
    return pl.ds(pl.multiple_of(place * steps, steps), steps)


def predicted_of(kept, arriving, starts, squares, packed):
    steps, width = kept.shape[0] // 2, kept.shape[1]

    def kernel(starts_ref, kept_ref, *refs):
        sent_ref, total_ref, squares_ref = refs[-3:]
        rows = []
        for at in range(2):
            part = pl.ds(at * steps, steps)
            arrived = refs[0][part, :] if len(arriving) == 1 else refs[at][...]
            total = kept_ref[part, :] + arrived.astype(F32)
            total_ref[part, :] = total
            rows.append(lane_sums(total))
        sent_ref[pl.ds(0, steps), :] = total_ref[half_of(1 - starts_ref[7, 0], steps), :].astype(BF16)
        both = jnp.concatenate(rows, axis=0)
        if squares is not None:
            both += refs[len(arriving)][...]
        squares_ref[...] = both
        if packed:
            sent_ref[pl.ds(steps, 16), :] = split(both, width)

    shapes = [
        in_vmem((steps + 16 * packed, width), BF16),
        in_vmem((2 * steps, width), F32),
        in_vmem((2, steps), F32),
    ]
    more = [] if squares is None else [squares]
    operands = [starts, kept, *arriving, *more]
    return call(kernel, shapes, [VMEM] * len(operands), name="predicted")(*operands)


def sum_of(total, arriving, starts, squares, packed, out_packed):
    steps, width = arriving.shape[0] - 16 * packed, arriving.shape[1]

    def kernel(starts_ref, total_ref, arriving_ref, *refs):
        sent_ref, out_ref = refs[-2:] if squares is None else refs[1:3]
        held = total_ref[half_of(starts_ref[7, 0], steps), :] if total.shape[0] > steps else total_ref[...]
        out = held + arriving_ref[pl.ds(0, steps), :].astype(F32)
        sent_ref[pl.ds(0, steps), :] = out.astype(BF16)
        out_ref[...] = out
        if squares is None:
            return
        both = refs[0][...]
        if packed:
            both += joined(arriving_ref[pl.ds(steps, 16), :], both.shape[1])
        refs[3][...] = both
        if out_packed:
            sent_ref[pl.ds(steps, 16), :] = split(both, width)

    shapes = [
        in_vmem((steps + 16 * out_packed, width), BF16),
        in_vmem((steps, width), F32),
    ]
    more = [] if squares is None else [squares]
    shapes += [in_vmem(value.shape, F32) for value in more]
    return call(kernel, shapes, [VMEM] * (3 + len(more)), name="sum_of")(
        starts, total, arriving, *more
    )


def kept_gradient(total, predicted, starts, cotangents, members, factor):
    steps, width = total.shape

    def kernel(starts_ref, total_ref, predicted_ref, own, other, grad_ref):
        first = starts_ref[7, 0] == 0
        weighting = jnp.where(first, own[:, :1], other[:, :1]).astype(F32) * factor
        predicted_rows = predicted_ref[half_of(starts_ref[7, 0], steps), :]
        grad_ref[...] = (weighting * (predicted_rows - total_ref[...] / members)).astype(BF16)

    operands = [starts, total, predicted, *cotangents]
    return call(
        kernel,
        in_vmem((steps, width), BF16),
        [VMEM] * len(operands),
        name="kept_gradient",
    )(*operands)


def gradient_of(total, arriving, predicted, starts, cotangents, members, factor, sums):
    steps, width = total.shape
    squares, previous, packed = sums

    def kernel(starts_ref, total_ref, arriving_ref, predicted_ref, own, other, *refs):
        refs, mean_ref = list(refs[:-1]), refs[-1]
        previous_ref = refs.pop(0) if previous is not None else None
        squares_ref = refs.pop(0) if squares is not None else None
        sent_ref, grad_ref, sums_ref = refs
        mean_ref[half_of(starts_ref[7, 0], steps), :] = total_ref[...] / members
        mean_ref[half_of(1 - starts_ref[7, 0], steps), :] = arriving_ref[...].astype(F32) / members
        rows = []
        for at, cotangent_ref in enumerate((own, other)):
            part = pl.ds(at * steps, steps)
            mean = mean_ref[part, :]
            weighting = cotangent_ref[:, :1].astype(F32) * factor
            grad_ref[part, :] = (weighting * (predicted_ref[part, :] - mean)).astype(BF16)
            rows.append(lane_sums(mean))
        sent_ref[pl.ds(0, steps), :] = grad_ref[half_of(1 - starts_ref[7, 0], steps), :]
        both = jnp.concatenate(rows, axis=0)
        if previous is not None:
            both += previous_ref[...]
        if squares is not None:
            both = squares_ref[...] / members - both
        sums_ref[...] = both
        if packed:
            sent_ref[pl.ds(steps, 16), :] = split(both, width)

    operands = [starts, total, arriving, predicted, *cotangents]
    operands += [value for value in (previous, squares) if value is not None]
    return call(
        kernel,
        [
            in_vmem((steps + 16 * packed, width), BF16),
            in_vmem((2 * steps, width), BF16),
            in_vmem((2, steps), F32),
        ],
        [VMEM] * len(operands),
        [pltpu.VMEM((2 * steps, width), F32)],
        name="gradient",
    )(*operands)


def in_place(kept, rest, starts, steps):
    def kernel(starts_ref, kept_ref, rest_ref, out_ref):
        out_ref[half_of(starts_ref[7, 0], steps), :] = kept_ref[...]
        out_ref[half_of(1 - starts_ref[7, 0], steps), :] = rest_ref[pl.ds(0, steps), :]

    out_shape = in_vmem((2 * steps, kept.shape[1]), BF16)
    return call(kernel, out_shape, [VMEM] * 3, name="in_place")(starts, kept, rest)


def plus(first, second):
    def kernel(first_ref, second_ref, out_ref):
        out_ref[...] = first_ref[...] + second_ref[...]

    return call(kernel, in_vmem(first.shape, F32), [VMEM, VMEM], name="plus")(first, second)


def leave_to_other(first, second, before, spread, arriving_spread, steps):
    units = before.shape[1]
    packed = arriving_spread.shape[0] > 2

    def kernel(g0, rows0, g1, rows1, before_ref, spread_ref, arriving_ref, out_ref, sum_ref):
        for span in cuts(units, 4):
            total = before_ref[:, span]
            for grad, rows in ((g0, rows0), (g1, rows1)):
                total += jnp.dot(
                    grad[pl.ds(steps, steps), :], rows[:, span], preferred_element_type=F32
                )
            out_ref[pl.ds(0, steps), span] = total.astype(BF16)
        if packed:
            both = spread_ref[...] + joined(arriving_ref[pl.ds(steps, 16), :], steps)
        else:
            both = spread_ref[...] + arriving_ref[...]
        sum_ref[...] = both
        out_ref[pl.ds(steps, 16), :] = split(both, units)

    shapes = [in_vmem((steps + 16, units), BF16), in_vmem((2, steps), F32)]
    return call(kernel, shapes, [VMEM] * 7, name="leave_to_other")(
        *first, *second, before, spread, arriving_spread
    )


def block_rows(grad, hidden, steps, rows):
    total = None
    for at, held in enumerate(hidden):
        term = lax.dot_general(
            grad[pl.ds(at * steps, steps), rows], held[...], TN, preferred_element_type=F32
        )
        total = term if total is None else total + term
    return total.astype(BF16)


def write_rows(start, grad, hidden, steps, made, out_ref, sems):
    copies = []
    for at, rows in enumerate(cuts(made.shape[0], 2)):
        made[rows, :] = block_rows(grad, hidden, steps, rows)
        to = pl.ds(pl.multiple_of(start + rows.start, rows.size), rows.size)
        copies.append(start_copy(made.at[rows, :], out_ref.at[to, :], sems.at[at]))
    return copies


def add_back(refs, pairs, added, sum_ref, part):
    steps, units = sum_ref.shape
    for span in cuts(units, 4):
        out = refs[2 * pairs][:, span] if added else None
        for at in range(pairs):
            grad, rows = refs[2 * at : 2 * at + 2]
            term = jnp.dot(
                grad[pl.ds(part * steps, steps), :], rows[:, span], preferred_element_type=F32
            )
            out = term if out is None else out + term
        sum_ref[:, span] = out


def weight_rows(grads, hidden, starts, blocks, features, started=None, back=()):
    half, (steps, units) = grads[0].shape[1], hidden[0].shape
    started = [] if started is None else [started]
    operands = []
    for _, pairs, before in back:
        operands += [value for pair in pairs for value in pair]
        operands += [] if before is None else [before]
    count = len(grads)

    def kernel(starts_ref, *refs):
        grad_refs, held, refs = refs[:count], refs[count : count + 2], refs[count + 2 :]
        out_ref, *sum_refs, made, sems = refs[len(operands) + len(started) :]
        copies = []
        for at, (grad, block) in enumerate(zip(grad_refs, blocks)):
            copies += write_rows(
                starts_ref[block, 0], grad, held, steps, made.at[at], out_ref, sems.at[at]
            )
        for (part, pairs, before), sum_ref in zip(back, sum_refs):
            add_back(refs, len(pairs), before is not None, sum_ref, part)
            refs = refs[2 * len(pairs) + (before is not None) :]
        for copy in copies:
            copy.wait()

    return call(
        kernel,
        [in_hbm((features, units), BF16)] + [in_vmem((steps, units), F32)] * len(back),
        [VMEM] * (3 + count + len(operands)) + [HBM] * len(started),
        [pltpu.VMEM((count, half, units), BF16), pltpu.SemaphoreType.DMA((count, 2))],
        aliases={3 + count + len(operands): 0} if started else None,
        name="weight_rows",
    )(starts, *grads, *hidden, *operands, *started)


def slope_of(pre_act):
    def kernel(pre, slope_ref):
        for span in cuts(pre_act.shape[1], 4):
            wide = pre[:, span].astype(F32)
            gate = sigmoid(wide)
            slope_ref[:, span] = gate * (1.0 + wide * (1.0 - gate))

    return call(kernel, in_vmem(pre_act.shape, F32), [VMEM], name="slope_of")(pre_act)


def last_grads(before, arrived, slope, spread, model_width):
    steps, units = before.shape
    lanes = -(-steps // 128) * 128

    def kernel(
        before_ref, arrived_ref, slope, spread_ref, act_ref, reward_ref, act, reward, sems
    ):
        others = joined(arrived_ref[pl.ds(steps, 16), pl.ds(0, lanes)], steps)
        reward[...] = (spread_ref[...][:1] + others[1:]) / model_width
        copies = [start_copy(reward, reward_ref, sems.at[4])]
        for at, span in enumerate(cuts(units, 4)):
            total = before_ref[:, span] + arrived_ref[pl.ds(0, steps), span].astype(F32)
            act[:, span] = (total * slope[:, span]).astype(BF16)
            copies.append(start_copy(act.at[:, span], act_ref.at[:, span], sems.at[at]))
        for copy in copies:
            copy.wait()

    return call(
        kernel,
        [in_hbm((steps, units), BF16), in_hbm((1, steps), F32)],
        [VMEM] * 4,
        [
            pltpu.VMEM((steps, units), BF16),
            pltpu.VMEM((1, steps), F32),
            pltpu.SemaphoreType.DMA((5,)),
        ],
        name="last_grads",
    )(before, arrived, slope, spread)


class Order:
    def __init__(self):
        self.last = None

    def __call__(self, step, *values):
        if self.last is not None:
            values, _ = lax.optimization_barrier((values, self.last))
        result = step(*values)
        self.last = jax.tree.leaves(result)[0]
        return result


class Piece:
    def __init__(self, order, starts, last, previous):
        self.order, self.starts = order, starts
        self.last, self.previous = last, previous
        self.tensor = lax.axis_index("tensor")
        self.arriving = []

    def leave(self, sent):
        self.arriving.append(swap(sent, "tensor", shares(lax.axis_size("tensor"))[-1]))

    def scatter_rest(self):
        def add(total, arriving):
            return total + arriving.astype(F32)

        for distance in reversed(shares(lax.axis_size("tensor"))[:-1]):
            half = self.total.shape[1] // 2
            high = (self.tensor // distance) % 2
            total = self.order(add, self.total, jnp.concatenate(self.arriving))
            sent = lax.dynamic_slice_in_dim(total, (1 - high) * half, half, 1)
            self.total = lax.dynamic_slice_in_dim(total, high * half, half, 1)
            self.arriving = [swap(sent.astype(BF16), "tensor", distance)]

    def predict(self):
        steps, width = self.total.shape[0] // 2, self.total.shape[1]
        self.packed = self.last and width >= steps
        before = None if self.previous is None else self.previous.squares
        sent, self.predicted, self.squares = self.order(
            lambda kept, *arriving: predicted_of(
                kept, arriving, self.starts, before, self.packed
            ),
            self.total,
            *self.arriving,
        )
        self.sum = self.predicted
        near, *self.far = shares(lax.axis_size("ensemble"))
        self.arriving = swap(sent, "ensemble", near)
        self.exchange_squares(near)

    def exchange_squares(self, distance):
        self.squares_arriving = None
        if self.last and not self.packed:
            self.squares_arriving = swap(self.squares, "ensemble", distance)

    def ensemble_steps(self):
        packed = self.packed
        for distance in self.far + [None]:
            out_packed = self.packed and distance is not None
            before = self.squares if self.last else None
            sent, self.sum, *squares = self.order(
                lambda total, arriving: sum_of(
                    total, arriving, self.starts, before, packed, out_packed
                ),
                self.sum,
                self.arriving,
            )
            if self.last:
                self.squares = squares[0]
            if self.squares_arriving is not None:
                self.squares = self.order(plus, self.squares, self.squares_arriving)
            if distance is not None:
                self.arriving = swap(sent, "ensemble", distance)
                self.exchange_squares(distance)
                yield
            else:
                self.arriving = swap(sent, "ensemble", 1)

    def gather(self, share):
        def join(share, other, distance):
            high = (self.tensor // distance) % 2
            first = jnp.where(high == 0, share, other)
            second = jnp.where(high == 0, other, share)
            return jnp.concatenate([first, second], axis=1)

        *near, far = shares(lax.axis_size("tensor"))
        for distance in near:
            other = swap(share, "tensor", distance)
            share = self.order(functools.partial(join, distance=distance), share, other)
        return share, swap(share, "tensor", far)

    def early_gradient(self, cotangents, members, factor):
        grad = self.order(
            lambda total: kept_gradient(
                total, self.predicted, self.starts, cotangents, members, factor
            ),
            self.sum,
        )
        self.kept = self.gather(grad)

    def gradient(self, cotangents, members, factor):
        *near, far = shares(lax.axis_size("tensor"))
        packed = self.last and not near and self.sum.shape[1] >= self.sum.shape[0]
        sums = (
            self.squares if self.last else None,
            None if self.previous is None else self.previous.sums,
            packed,
        )
        sent, self.share, self.sums = self.order(
            lambda total, arriving: gradient_of(
                total,
                arriving,
                self.predicted,
                self.starts,
                cotangents,
                members,
                factor,
                sums,
            ),
            self.sum,
            self.arriving,
        )
        self.rest = self.gather(sent)
        self.other_sums = self.rest[1]
        if self.last and not packed:
            for distance in near:
                self.sums = self.order(plus, self.sums, swap(self.sums, "tensor", distance))
            self.other_sums = swap(self.sums, "tensor", far)
        if near:
            self.share = self.together(0)

    def together(self, which):
        steps = self.sum.shape[0]
        return self.order(
            lambda kept, rest: in_place(kept, rest, self.starts, steps),
            self.kept[which],
            self.rest[which],
        )


def body(pre_act, weights, cotangent):
    pre_act, weights = pre_act[:, 0, :], weights[0]
    steps, features = pre_act.shape[0], weights.shape[0]
    members = lax.axis_size("ensemble")
    model_width = features * lax.axis_size("seq")
    factor = 2.0 / (members * model_width)
    half = features // (2 * PIECES)
    far = shares(lax.axis_size("tensor"))[-1]
    high = (lax.axis_index("tensor") // far) % 2
    starts = []
    for piece in range(PIECES):
        starts += [(2 * piece + 1 - high) * half, (2 * piece + high) * half]
    assert len(starts) < 8
    starts += [0] * (7 - len(starts)) + [lax.axis_index("ensemble") % 2]
    starts = jnp.broadcast_to(jnp.stack(starts).astype(jnp.int32)[:, None], (8, 128))

    pre_other = swap(pre_act, "seq", 1)
    cot_other = swap(cotangent, "seq", 1)
    pre_act, starts = lax.optimization_barrier((pre_act, starts))
    order = Order()
    pieces = []
    for at in range(PIECES):
        previous = pieces[-1] if pieces else None
        pieces.append(Piece(order, starts, at == PIECES - 1, previous))
    blocks = [None] * (2 * PIECES)
    sent, hidden, blocks[0], pre_act = order(
        lambda p: load_first(p, weights, starts, half), pre_act
    )
    pieces[0].leave(sent)
    sent, hidden_other, blocks[2] = order(
        lambda p: load_second(p, weights, starts, blocks[0], 2), pre_other
    )
    pieces[0].leave(sent)
    both = [hidden, hidden_other]

    def products(at, following):
        out = order(
            lambda rows: project(
                both, rows, F32 if at % 2 else BF16, weights, starts, following
            ),
            blocks[at],
        )
        if following is not None:
            blocks[following] = out[1]
        return out[0]

    a, b = pieces
    b.leave(products(2, 1))
    a.total = products(1, 3)
    a.scatter_rest()
    a.predict()
    b.total = products(3, None)
    slope = order(slope_of, pre_act)
    cotangents = [
        order(lambda c: jnp.broadcast_to(c[:, None], (steps, 128)), value)
        for value in (cotangent, cot_other)
    ]
    b.scatter_rest()
    b.predict()
    a_steps, b_steps = a.ensemble_steps(), b.ensemble_steps()
    next(a_steps)
    for _ in b.far:
        next(b_steps)
        next(a_steps, None)
    a.early_gradient(cotangents, members, factor)
    next(b_steps, None)
    b.early_gradient(cotangents, members, factor)
    a.gradient(cotangents, members, factor)

    def rows_of(shares, at, started, back):
        return order(
            lambda started, *shares: weight_rows(
                shares,
                both,
                starts,
                at,
                features,
                started,
                [
                    (part, [(shares[n], blocks[at[n]]) for n in range(len(at))], before)
                    for part, before in back
                ],
            ),
            started,
            *shares,
        )

    sides = [(1, None), (0, None)]
    weight_grads, before_other, before = rows_of([a.share], [1], None, sides)
    b.gradient(cotangents, members, factor)
    sides = [(1, before_other), (0, before)]
    weight_grads, before_other, before = rows_of([b.share], [3], weight_grads, sides)
    a_other = a.together(1)
    b_other = b.together(1)
    leaving, spread = order(
        lambda x, y, z: leave_to_other(
            (x, blocks[0]), (y, blocks[2]), before_other, b.sums, z, steps
        ),
        a_other,
        b_other,
        b.other_sums,
    )
    arrived = swap(leaving, "seq", 1)
    weight_grads, before = rows_of([a_other, b_other], [0, 2], weight_grads, [(0, before)])
    act_grads, reward = order(
        lambda g, s: last_grads(g, s, slope, spread, model_width), before, arrived
    )
    return (weight_grads[None], act_grads[:, None, :], reward[0])


def solution(mesh):
    placed = (
        P(("groups", "seq"), "ensemble", "tensor"),
        P("ensemble", "seq", "tensor"),
        P(("groups", "seq")),
    )
    return jax.shard_map(
        body,
        mesh=mesh,
        in_specs=placed,
        out_specs=(
            P(("groups", "ensemble"), "seq", "tensor"),
            P(("groups", "seq"), "ensemble", "tensor"),
            P(("groups", "seq")),
        ),
        check_vma=False,
    )
```

```python
import functools

import jax
import jax.numpy as jnp
from jax import lax
from jax.experimental import pallas as pl
from jax.experimental.pallas import tpu as pltpu
from jax.sharding import PartitionSpec as P

F32, BF16 = jnp.float32, jnp.bfloat16
NT = (((1,), (1,)), ((), ()))
TN = (((0,), (0,)), ((), ()))
PIECES = 2
WORK = 0.45
VMEM_LIMIT = 16 * 2**20


def swap(value, axis, distance):
    size = lax.axis_size(axis)
    return lax.ppermute(value, axis, [(i, i ^ distance) for i in range(size)])


def shares(size):
    return [1 << bit for bit in range(size.bit_length() - 1)]


def sigmoid(wide):
    return jax.nn.sigmoid(wide)


def silu(value):
    wide = value.astype(F32)
    return (wide * sigmoid(wide)).astype(BF16)


VMEM = pl.BlockSpec(memory_space=pltpu.VMEM)
HBM = pl.BlockSpec(memory_space=pltpu.HBM)


def in_vmem(shape, dtype):
    return pltpu.VMEM(shape, dtype)


def in_hbm(shape, dtype):
    return pltpu.HBM(shape, dtype)


def call(kernel, out_shape, in_specs, scratch=(), aliases=None, name=None):
    outs = out_shape if isinstance(out_shape, list) else [out_shape]
    out_specs = [pl.BlockSpec(memory_space=out.memory_space) for out in outs]
    run = pl.pallas_call(
        kernel,
        out_shape=outs,
        in_specs=in_specs,
        out_specs=out_specs,
        scratch_shapes=list(scratch),
        input_output_aliases=aliases or {},
        compiler_params=pltpu.CompilerParams(vmem_limit_bytes=VMEM_LIMIT),
        cost_estimate=pl.CostEstimate(
            flops=int(WORK * 1e9), bytes_accessed=1, transcendentals=0
        ),
        name=name,
    )

    def placed(*operands):
        operands = [
            pltpu.with_memory_space_constraint(value, spec.memory_space)
            for value, spec in zip(operands, in_specs)
        ]
        result = run(*operands)
        return result if isinstance(out_shape, list) else result[0]

    return placed


def cuts(whole, parts):
    return [pl.ds(at * (whole // parts), whole // parts) for at in range(parts)]


def number(numbers_ref, at, step):
    return pl.multiple_of(numbers_ref[at, 0], step)


def start_copy(source, target, sem):
    copy = pltpu.make_async_copy(source, target, sem)
    copy.start()
    return copy


def split(rows, width):
    count, steps = rows.shape
    parts = []
    for _ in range(3):
        part = rows.astype(BF16).astype(F32)
        parts.append(part)
        rows = rows - part
    parts.append(jnp.zeros((16 - 3 * count, steps), F32))
    out = jnp.concatenate(parts, axis=0)
    if width > steps:
        out = jnp.concatenate([out, jnp.zeros((16, width - steps), F32)], axis=1)
    return out.astype(BF16)


def joined(parts, steps):
    wide = parts[:, :steps].astype(F32)
    return wide[:2] + wide[2:4] + wide[4:6]


def load_first(source, weights, starts, half):
    steps, units = source.shape
    spans = 4
    width = units // spans

    def kernel(starts_ref, source_ref, weights_ref, sent_ref, hidden_ref, *refs):
        held, following, pre, total, sems, sem = refs
        rows = pl.ds(number(starts_ref, 0, half), half)
        later = pl.ds(number(starts_ref, 2, half), half)

        def copies(at):
            span = pl.ds(pl.multiple_of(at * width, width), width)
            return span, (
                pltpu.make_async_copy(source_ref.at[:, span], pre.at[:, span], sems.at[0, at]),
                pltpu.make_async_copy(
                    weights_ref.at[rows, span], held.at[:, span], sems.at[1, at]
                ),
            )

        def start(at):
            for copy in copies(at)[1]:
                copy.start()

        for at in range(spans):
            start(at)
        copy = start_copy(weights_ref.at[later, :], following, sem)
        total[...] = jnp.zeros_like(total)

        def step(at, carry):
            span, pair = copies(at)
            for copy in pair:
                copy.wait()
            hidden = silu(pre[:, span])
            hidden_ref[pl.ds(0, steps), span] = hidden
            total[...] += lax.dot_general(
                hidden, held[:, span], NT, preferred_element_type=F32
            )
            return carry

        lax.fori_loop(0, spans, step, 0)
        sent_ref[...] = total[...].astype(BF16)
        copy.wait()

    return call(
        kernel,
        [
            in_vmem((steps, half), BF16),
            in_vmem((2 * steps, units), BF16),
            in_vmem((half, units), BF16),
            in_vmem((half, units), BF16),
            in_vmem((steps, units), BF16),
        ],
        [VMEM, HBM, HBM],
        [
            pltpu.VMEM((steps, half), F32),
            pltpu.SemaphoreType.DMA((2, spans)),
            pltpu.SemaphoreType.DMA,
        ],
        name="load_first",
    )(starts, source, weights)


def load_second(source, weights, starts, held, hidden, following):
    steps, units = source.shape
    half = held.shape[0]

    def kernel(
        starts_ref, source_ref, weights_ref, held_ref, _, out_ref, hidden_ref, block, sem
    ):
        first = number(starts_ref, following, half)
        copy = start_copy(weights_ref.at[pl.ds(first, half), :], block, sem)

        @pl.when(first >= 0)
        def _():
            total = None
            for span in cuts(units, 4):
                hidden = silu(source_ref[:, span])
                hidden_ref[pl.ds(steps, steps), span] = hidden
                term = lax.dot_general(hidden, held_ref[:, span], NT, preferred_element_type=F32)
                total = term if total is None else total + term
            out_ref[...] = total.astype(BF16)

        copy.wait()

    return call(
        kernel,
        [
            in_vmem((steps, half), BF16),
            in_vmem((2 * steps, units), BF16),
            in_vmem((half, units), BF16),
        ],
        [VMEM, VMEM, HBM, VMEM, VMEM],
        [pltpu.SemaphoreType.DMA],
        aliases={4: 1},
        name="load_second",
    )(starts, source, weights, held, hidden)


def project(hidden, rows, out_type, weights, starts, following):
    steps, units = hidden.shape
    half = rows.shape[0]

    def product(hidden_ref, rows_ref, out_ref):
        total = lax.dot_general(hidden_ref[...], rows_ref[...], NT, preferred_element_type=F32)
        out_ref[...] = total.astype(out_type)

    def loading(starts_ref, weights_ref, hidden_ref, rows_ref, out_ref, block, sem):
        start = number(starts_ref, following, half)
        copy = start_copy(weights_ref.at[pl.ds(start, half), :], block, sem)

        @pl.when(start >= 0)
        def _():
            product(hidden_ref, rows_ref, out_ref)

        copy.wait()

    out_shape = in_vmem((steps, half), out_type)
    if following is None:
        return [call(product, out_shape, [VMEM] * 2, name="project")(hidden, rows)]
    return call(
        loading,
        [out_shape, in_vmem((half, units), BF16)],
        [VMEM, HBM, VMEM, VMEM],
        [pltpu.SemaphoreType.DMA],
        name="project",
    )(starts, weights, hidden, rows)


def lane_sums(value):
    width = value.shape[1]
    if width % 128 == 0:
        squares = value * value
        squares = sum(squares[:, at : at + 128] for at in range(0, width, 128))
        return jnp.sum(squares.T, axis=0, keepdims=True)
    ones = jnp.ones((8, value.shape[1]), F32)
    sums = lax.dot_general(
        ones, value * value, NT, precision=lax.Precision.HIGHEST, preferred_element_type=F32
    )
    return sums[:1]


def half_of(place, steps):
    return pl.ds(pl.multiple_of(place * steps, steps), steps)


def predicted_of(kept, arriving, starts, squares, packed):
    steps, width = kept.shape[0] // 2, kept.shape[1]

    def kernel(starts_ref, kept_ref, *refs):
        sent_ref, total_ref, squares_ref = refs[-3:]
        rows = []
        for at in range(2):
            part = pl.ds(at * steps, steps)
            arrived = refs[0][part, :] if len(arriving) == 1 else refs[at][...]
            total = kept_ref[part, :] + arrived.astype(F32)
            total_ref[part, :] = total
            rows.append(lane_sums(total))
        sent_ref[pl.ds(0, steps), :] = total_ref[half_of(1 - starts_ref[7, 0], steps), :].astype(BF16)
        both = jnp.concatenate(rows, axis=0)
        if squares is not None:
            both += refs[len(arriving)][...]
        squares_ref[...] = both
        if packed:
            sent_ref[pl.ds(steps, 16), :] = split(both, width)

    shapes = [
        in_vmem((steps + 16 * packed, width), BF16),
        in_vmem((2 * steps, width), F32),
        in_vmem((2, steps), F32),
    ]
    more = [] if squares is None else [squares]
    operands = [starts, kept, *arriving, *more]
    return call(kernel, shapes, [VMEM] * len(operands), name="predicted")(*operands)


def sum_of(total, arriving, starts, squares, packed, out_packed):
    steps, width = arriving.shape[0] - 16 * packed, arriving.shape[1]

    def kernel(starts_ref, total_ref, arriving_ref, *refs):
        sent_ref, out_ref = refs[-2:] if squares is None else refs[1:3]
        held = total_ref[half_of(starts_ref[7, 0], steps), :] if total.shape[0] > steps else total_ref[...]
        out = held + arriving_ref[pl.ds(0, steps), :].astype(F32)
        sent_ref[pl.ds(0, steps), :] = out.astype(BF16)
        out_ref[...] = out
        if squares is None:
            return
        both = refs[0][...]
        if packed:
            both += joined(arriving_ref[pl.ds(steps, 16), :], both.shape[1])
        refs[3][...] = both
        if out_packed:
            sent_ref[pl.ds(steps, 16), :] = split(both, width)

    shapes = [
        in_vmem((steps + 16 * out_packed, width), BF16),
        in_vmem((steps, width), F32),
    ]
    more = [] if squares is None else [squares]
    shapes += [in_vmem(value.shape, F32) for value in more]
    return call(kernel, shapes, [VMEM] * (3 + len(more)), name="sum_of")(
        starts, total, arriving, *more
    )


def kept_gradient(total, predicted, starts, cotangents, members, factor):
    steps, width = total.shape

    def kernel(starts_ref, total_ref, predicted_ref, own, other, grad_ref):
        first = starts_ref[7, 0] == 0
        weighting = jnp.where(first, own[:, :1], other[:, :1]).astype(F32) * factor
        predicted_rows = predicted_ref[half_of(starts_ref[7, 0], steps), :]
        grad_ref[...] = (weighting * (predicted_rows - total_ref[...] / members)).astype(BF16)

    operands = [starts, total, predicted, *cotangents]
    return call(
        kernel,
        in_vmem((steps, width), BF16),
        [VMEM] * len(operands),
        name="kept_gradient",
    )(*operands)


def gradient_of(total, arriving, predicted, starts, cotangents, members, factor, sums, passed):
    steps, width = total.shape
    squares, previous, packed = sums

    def kernel(starts_ref, total_ref, arriving_ref, predicted_ref, own, other, *refs):
        refs, mean_ref = list(refs[:-1]), refs[-1]
        previous_ref = refs.pop(0) if previous is not None else None
        squares_ref = refs.pop(0) if squares is not None else None
        if passed is not None:
            passed_ref = refs.pop(0)
            refs[0][pl.ds(steps, steps), :] = passed_ref[...]
        sent_ref, grad_ref, sums_ref = refs
        mean_ref[half_of(starts_ref[7, 0], steps), :] = total_ref[...] / members
        mean_ref[half_of(1 - starts_ref[7, 0], steps), :] = arriving_ref[...].astype(F32) / members
        rows = []
        for at, cotangent_ref in enumerate((own, other)):
            part = pl.ds(at * steps, steps)
            mean = mean_ref[part, :]
            weighting = cotangent_ref[:, :1].astype(F32) * factor
            grad_ref[part, :] = (weighting * (predicted_ref[part, :] - mean)).astype(BF16)
            rows.append(lane_sums(mean))
        sent_ref[pl.ds(0, steps), :] = grad_ref[half_of(1 - starts_ref[7, 0], steps), :]
        both = jnp.concatenate(rows, axis=0)
        if previous is not None:
            both += previous_ref[...]
        if squares is not None:
            both = squares_ref[...] / members - both
        sums_ref[...] = both
        if packed:
            sent_ref[pl.ds(steps, 16), :] = split(both, width)

    operands = [starts, total, arriving, predicted, *cotangents]
    operands += [value for value in (previous, squares, passed) if value is not None]
    below = 16 * packed if passed is None else steps
    return call(
        kernel,
        [
            in_vmem((steps + below, width), BF16),
            in_vmem((2 * steps, width), BF16),
            in_vmem((2, steps), F32),
        ],
        [VMEM] * len(operands),
        [pltpu.VMEM((2 * steps, width), F32)],
        name="gradient",
    )(*operands)


def in_place(kept, rest, starts, steps, offset):
    def kernel(starts_ref, kept_ref, rest_ref, out_ref):
        out_ref[half_of(starts_ref[7, 0], steps), :] = kept_ref[pl.ds(offset, steps), :]
        out_ref[half_of(1 - starts_ref[7, 0], steps), :] = rest_ref[pl.ds(0, steps), :]

    out_shape = in_vmem((2 * steps, kept.shape[1]), BF16)
    return call(kernel, out_shape, [VMEM] * 3, name="in_place")(starts, kept, rest)


def plus(first, second):
    def kernel(first_ref, second_ref, out_ref):
        out_ref[...] = first_ref[...] + second_ref[...]

    return call(kernel, in_vmem(first.shape, F32), [VMEM, VMEM], name="plus")(first, second)


def leave_to_other(first, second, before, spread, arriving_spread, steps):
    units = before.shape[1]
    packed = arriving_spread.shape[0] > 2

    def kernel(g0, rows0, g1, rows1, before_ref, spread_ref, arriving_ref, out_ref, sum_ref):
        for span in cuts(units, 4):
            total = before_ref[pl.ds(steps, steps), span]
            for grad, rows in ((g0, rows0), (g1, rows1)):
                total += jnp.dot(
                    grad[pl.ds(steps, steps), :], rows[:, span], preferred_element_type=F32
                )
            out_ref[pl.ds(0, steps), span] = total.astype(BF16)
        if packed:
            both = spread_ref[...] + joined(arriving_ref[pl.ds(steps, 16), :], steps)
        else:
            both = spread_ref[...] + arriving_ref[...]
        sum_ref[...] = both
        out_ref[pl.ds(steps, 16), :] = split(both, units)

    shapes = [in_vmem((steps + 16, units), BF16), in_vmem((2, steps), F32)]
    return call(kernel, shapes, [VMEM] * 7, name="leave_to_other")(
        *first, *second, before, spread, arriving_spread
    )


def send_block(made, at, span, starts_ref, block, out_ref, sem):
    half = made.shape[1]
    to = pl.ds(number(starts_ref, block, half), half)
    return start_copy(made.at[at, :, span], out_ref.at[to, span], sem)


def kept_products(kept, hidden, rows, starts):
    (steps, half), units = kept.shape, rows.shape[1]

    def kernel(starts_ref, kept_ref, h, rows_ref, term_ref, back_ref):
        part = half_of(starts_ref[7, 0], steps)
        for span in cuts(units, 4):
            term = lax.dot_general(kept_ref[...], h[part, span], TN, preferred_element_type=F32)
            term_ref[:, span] = term.astype(BF16)
            back_ref[:, span] = jnp.dot(
                kept_ref[...], rows_ref[:, span], preferred_element_type=F32
            )

    shapes = [in_vmem((half, units), BF16), in_vmem((steps, units), F32)]
    return call(kernel, shapes, [VMEM] * 4, name="kept_products")(starts, kept, hidden, rows)


def first_blocks(first, second, term, hidden, starts, blocks, features, rows, kept_back):
    half, (steps, units) = first.shape[1], kept_back.shape

    def kernel(starts_ref, g0, g1, term_ref, h, w0, w1, kept_ref, out_ref, sum_ref, made, sems):
        kept, rest = half_of(starts_ref[7, 0], steps), half_of(1 - starts_ref[7, 0], steps)
        copies = []
        for at, span in enumerate(cuts(units, 4)):
            total = lax.dot_general(g1[...], h[:, span], TN, preferred_element_type=F32)
            made[1, :, span] = total.astype(BF16)
            copies.append(
                send_block(made, 1, span, starts_ref, blocks[1], out_ref, sems.at[1, at])
            )
        for at, span in enumerate(cuts(units, 4)):
            total = lax.dot_general(g0[rest, :], h[rest, span], TN, preferred_element_type=F32)
            made[0, :, span] = (total + term_ref[:, span].astype(F32)).astype(BF16)
            copies.append(
                send_block(made, 0, span, starts_ref, blocks[0], out_ref, sems.at[0, at])
            )
        for span in cuts(units, 4):
            for part, more in ((kept, kept_ref), (rest, None)):
                total = jnp.dot(g1[part, :], w1[:, span], preferred_element_type=F32)
                if more is None:
                    total += jnp.dot(g0[part, :], w0[:, span], preferred_element_type=F32)
                else:
                    total += more[:, span]
                sum_ref[part, span] = total
        for copy in copies:
            copy.wait()

    return call(
        kernel,
        [in_hbm((features, units), BF16), in_vmem((2 * steps, units), F32)],
        [VMEM] * 8,
        [pltpu.VMEM((2, half, units), BF16), pltpu.SemaphoreType.DMA((2, 4))],
        name="first_blocks",
    )(starts, first, second, term, hidden, *rows, kept_back)


def last_blocks(grads, hidden, starts, blocks, started, rows, before):
    (features, units), half = started.shape, grads[0].shape[1]
    steps = before.shape[0] // 2

    def kernel(starts_ref, g0, g1, h, w0, w1, before_ref, _, out_ref, sum_ref, made, sems):
        copies = []
        for block, grad in enumerate((g0, g1)):
            for at, span in enumerate(cuts(units, 4)):
                total = lax.dot_general(grad[...], h[:, span], TN, preferred_element_type=F32)
                made[block, :, span] = total.astype(BF16)
                copies.append(
                    send_block(
                        made, block, span, starts_ref, blocks[block], out_ref, sems.at[block, at]
                    )
                )
        own = pl.ds(0, steps)
        for span in cuts(units, 4):
            total = jnp.dot(g0[own, :], w0[:, span], preferred_element_type=F32)
            total += jnp.dot(g1[own, :], w1[:, span], preferred_element_type=F32)
            sum_ref[:, span] = total + before_ref[own, span]
        for copy in copies:
            copy.wait()

    return call(
        kernel,
        [in_hbm((features, units), BF16), in_vmem((steps, units), F32)],
        [VMEM] * 7 + [HBM],
        [pltpu.VMEM((2, half, units), BF16), pltpu.SemaphoreType.DMA((2, 4))],
        aliases={7: 0},
        name="last_blocks",
    )(starts, *grads, hidden, *rows, before, started)


def slope_of(pre_act):
    def kernel(pre, slope_ref):
        for span in cuts(pre_act.shape[1], 4):
            wide = pre[:, span].astype(F32)
            gate = sigmoid(wide)
            slope_ref[:, span] = gate * (1.0 + wide * (1.0 - gate))

    return call(kernel, in_vmem(pre_act.shape, F32), [VMEM], name="slope_of")(pre_act)


def last_grads(before, arrived, slope, spread, model_width):
    steps, units = before.shape
    lanes = -(-steps // 128) * 128

    def kernel(
        before_ref, arrived_ref, slope, spread_ref, act_ref, reward_ref, act, reward, sems
    ):
        others = joined(arrived_ref[pl.ds(steps, 16), pl.ds(0, lanes)], steps)
        reward[...] = (spread_ref[...][:1] + others[1:]) / model_width
        copies = [start_copy(reward, reward_ref, sems.at[4])]
        for at, span in enumerate(cuts(units, 4)):
            total = before_ref[:, span] + arrived_ref[pl.ds(0, steps), span].astype(F32)
            act[:, span] = (total * slope[:, span]).astype(BF16)
            copies.append(start_copy(act.at[:, span], act_ref.at[:, span], sems.at[at]))
        for copy in copies:
            copy.wait()

    return call(
        kernel,
        [in_hbm((steps, units), BF16), in_hbm((1, steps), F32)],
        [VMEM] * 4,
        [
            pltpu.VMEM((steps, units), BF16),
            pltpu.VMEM((1, steps), F32),
            pltpu.SemaphoreType.DMA((5,)),
        ],
        name="last_grads",
    )(before, arrived, slope, spread)


class Order:
    def __init__(self):
        self.last = None

    def __call__(self, step, *values):
        if self.last is not None:
            values, _ = lax.optimization_barrier((values, self.last))
        result = step(*values)
        self.last = jax.tree.leaves(result)[0]
        return result


class Piece:
    def __init__(self, order, starts, last, previous):
        self.order, self.starts = order, starts
        self.last, self.previous = last, previous
        self.tensor = lax.axis_index("tensor")
        self.arriving = []

    def leave(self, sent):
        self.arriving.append(swap(sent, "tensor", shares(lax.axis_size("tensor"))[-1]))

    def scatter_rest(self):
        def add(total, arriving):
            return total + arriving.astype(F32)

        for distance in reversed(shares(lax.axis_size("tensor"))[:-1]):
            half = self.total.shape[1] // 2
            high = (self.tensor // distance) % 2
            total = self.order(add, self.total, jnp.concatenate(self.arriving))
            sent = lax.dynamic_slice_in_dim(total, (1 - high) * half, half, 1)
            self.total = lax.dynamic_slice_in_dim(total, high * half, half, 1)
            self.arriving = [swap(sent.astype(BF16), "tensor", distance)]

    def predict(self):
        steps, width = self.total.shape[0] // 2, self.total.shape[1]
        self.packed = self.last and width >= steps
        before = None if self.previous is None else self.previous.squares
        sent, self.predicted, self.squares = self.order(
            lambda kept, *arriving: predicted_of(
                kept, arriving, self.starts, before, self.packed
            ),
            self.total,
            *self.arriving,
        )
        self.sum = self.predicted
        near, *self.far = shares(lax.axis_size("ensemble"))
        self.arriving = swap(sent, "ensemble", near)
        self.exchange_squares(near)

    def exchange_squares(self, distance):
        self.squares_arriving = None
        if self.last and not self.packed:
            self.squares_arriving = swap(self.squares, "ensemble", distance)

    def ensemble_steps(self):
        packed = self.packed
        for distance in self.far + [None]:
            out_packed = self.packed and distance is not None
            before = self.squares if self.last else None
            sent, self.sum, *squares = self.order(
                lambda total, arriving: sum_of(
                    total, arriving, self.starts, before, packed, out_packed
                ),
                self.sum,
                self.arriving,
            )
            if self.last:
                self.squares = squares[0]
            if self.squares_arriving is not None:
                self.squares = self.order(plus, self.squares, self.squares_arriving)
            if distance is not None:
                self.arriving = swap(sent, "ensemble", distance)
                self.exchange_squares(distance)
                yield
            else:
                self.arriving = swap(sent, "ensemble", 1)

    def gather(self, share):
        def join(share, other, distance):
            high = (self.tensor // distance) % 2
            first = jnp.where(high == 0, share, other)
            second = jnp.where(high == 0, other, share)
            return jnp.concatenate([first, second], axis=1)

        *near, far = shares(lax.axis_size("tensor"))
        for distance in near:
            other = swap(share, "tensor", distance)
            share = self.order(functools.partial(join, distance=distance), share, other)
        return share, swap(share, "tensor", far)

    def early_gradient(self, cotangents, members, factor):
        return self.order(
            lambda total: kept_gradient(
                total, self.predicted, self.starts, cotangents, members, factor
            ),
            self.sum,
        )

    def gradient(self, cotangents, members, factor, passed=None):
        *near, far = shares(lax.axis_size("tensor"))
        packed = self.last and not near and self.sum.shape[1] >= self.sum.shape[0]
        sums = (
            self.squares if self.last else None,
            None if self.previous is None else self.previous.sums,
            packed,
        )
        sent, self.share, self.sums = self.order(
            lambda total, arriving: gradient_of(
                total,
                arriving,
                self.predicted,
                self.starts,
                cotangents,
                members,
                factor,
                sums,
                passed,
            ),
            self.sum,
            self.arriving,
        )
        self.rest = self.gather(sent)
        self.other_sums = self.rest[1]
        if self.last and not packed:
            for distance in near:
                self.sums = self.order(plus, self.sums, swap(self.sums, "tensor", distance))
            self.other_sums = swap(self.sums, "tensor", far)
        if near:
            self.share = self.together(0)

    def together(self, which):
        steps = self.sum.shape[0]
        return self.order(
            lambda kept, rest: in_place(kept, rest, self.starts, steps, self.offset),
            self.kept[which],
            self.rest[which],
        )


def body(pre_act, weights, cotangent):
    pre_act, weights = pre_act[:, 0, :], weights[0]
    steps, features = pre_act.shape[0], weights.shape[0]
    members = lax.axis_size("ensemble")
    model_width = features * lax.axis_size("seq")
    factor = 2.0 / (members * model_width)
    half = features // (2 * PIECES)
    far = shares(lax.axis_size("tensor"))[-1]
    high = (lax.axis_index("tensor") // far) % 2
    starts = []
    for piece in range(PIECES):
        starts += [(2 * piece + 1 - high) * half, (2 * piece + high) * half]
    assert len(starts) < 8
    starts += [0] * (7 - len(starts)) + [lax.axis_index("ensemble") % 2]
    starts = jnp.broadcast_to(jnp.stack(starts).astype(jnp.int32)[:, None], (8, 128))

    pre_other = swap(pre_act, "seq", 1)
    pre_act, starts = lax.optimization_barrier((pre_act, starts))
    order = Order()
    pieces = []
    for at in range(PIECES):
        previous = pieces[-1] if pieces else None
        pieces.append(Piece(order, starts, at == PIECES - 1, previous))
    blocks = [None] * (2 * PIECES)
    sent, hidden, blocks[0], blocks[2], pre_act = order(
        lambda p: load_first(p, weights, starts, half), pre_act
    )
    pieces[0].leave(sent)
    sent, hidden, blocks[1] = order(
        lambda p, h: load_second(p, weights, starts, blocks[0], h, 1), pre_other, hidden
    )
    pieces[0].leave(sent)

    def products(at, following):
        out = order(
            lambda rows: project(
                hidden, rows, F32 if at % 2 else BF16, weights, starts, following
            ),
            blocks[at],
        )
        if following is not None:
            blocks[following] = out[1]
        return out[0]

    a, b = pieces
    b.leave(products(2, 3))
    a.total = products(1, None)
    a.scatter_rest()
    a.predict()
    b.total = products(3, None)
    slope = order(slope_of, pre_act)
    cot_other = swap(order(lambda c: c, cotangent), "seq", 1)
    b.scatter_rest()
    b.predict()
    a_steps, b_steps = a.ensemble_steps(), b.ensemble_steps()
    next(a_steps)
    for _ in b.far:
        next(b_steps)
        next(a_steps, None)
    cotangents = [
        order(lambda c: jnp.broadcast_to(c[:, None], (steps, 128)), value)
        for value in (cotangent, cot_other)
    ]
    kept = a.early_gradient(cotangents, members, factor)
    a.kept, a.offset = a.gather(kept), 0
    rows_early, rows_late = [blocks[1], blocks[3]], [blocks[0], blocks[2]]
    next(b_steps, None)
    term, kept_back = order(
        lambda g: kept_products(g, hidden, blocks[1], starts), a.kept[0]
    )
    kept = b.early_gradient(cotangents, members, factor)
    a.kept = a.kept[0], order(lambda x: x, a.kept[1])
    a.gradient(cotangents, members, factor, kept)
    b.kept, b.offset = a.rest, steps
    b.gradient(cotangents, members, factor)
    weight_grads, before = order(
        lambda x, y: first_blocks(
            x, y, term, hidden, starts, [1, 3], features, rows_early, kept_back
        ),
        a.share,
        b.share,
    )
    a_other = a.together(1)
    b_other = b.together(1)
    leaving, spread = order(
        lambda x, y, z: leave_to_other(
            (x, blocks[0]), (y, blocks[2]), before, b.sums, z, steps
        ),
        a_other,
        b_other,
        b.other_sums,
    )
    arrived = swap(leaving, "seq", 1)
    weight_grads, before = order(
        lambda x, y, s: last_blocks([x, y], hidden, starts, [0, 2], s, rows_late, before),
        a_other,
        b_other,
        weight_grads,
    )
    act_grads, reward = order(
        lambda g, s: last_grads(g, s, slope, spread, model_width), before, arrived
    )
    return (weight_grads[None], act_grads[:, None, :], reward[0])


def solution(mesh):
    placed = (
        P(("groups", "seq"), "ensemble", "tensor"),
        P("ensemble", "seq", "tensor"),
        P(("groups", "seq")),
    )
    return jax.shard_map(
        body,
        mesh=mesh,
        in_specs=placed,
        out_specs=(
            P(("groups", "ensemble"), "seq", "tensor"),
            P(("groups", "seq"), "ensemble", "tensor"),
            P(("groups", "seq")),
        ),
        check_vma=False,
    )
```

```python
import functools

import jax
import jax.numpy as jnp
from jax import lax
from jax.experimental import pallas as pl
from jax.experimental.pallas import tpu as pltpu
from jax.sharding import PartitionSpec as P

F32, BF16 = jnp.float32, jnp.bfloat16
NT = (((1,), (1,)), ((), ()))
TN = (((0,), (0,)), ((), ()))
PIECES = 2
WORK = 0.4
VMEM_LIMIT = 16 * 2**20


def swap(value, axis, distance):
    size = lax.axis_size(axis)
    return lax.ppermute(value, axis, [(i, i ^ distance) for i in range(size)])


def shares(size):
    return [1 << bit for bit in range(size.bit_length() - 1)]


def sigmoid(wide):
    return jax.nn.sigmoid(wide)


def silu(value):
    wide = value.astype(F32)
    return (wide * sigmoid(wide)).astype(BF16)


VMEM = pl.BlockSpec(memory_space=pltpu.VMEM)
HBM = pl.BlockSpec(memory_space=pltpu.HBM)


def in_vmem(shape, dtype):
    return pltpu.VMEM(shape, dtype)


def in_hbm(shape, dtype):
    return pltpu.HBM(shape, dtype)


def call(kernel, out_shape, in_specs, scratch=(), aliases=None, work=WORK, name=None):
    outs = out_shape if isinstance(out_shape, list) else [out_shape]
    out_specs = [pl.BlockSpec(memory_space=out.memory_space) for out in outs]
    run = pl.pallas_call(
        kernel,
        out_shape=outs,
        in_specs=in_specs,
        out_specs=out_specs,
        scratch_shapes=list(scratch),
        input_output_aliases=aliases or {},
        compiler_params=pltpu.CompilerParams(vmem_limit_bytes=VMEM_LIMIT),
        cost_estimate=pl.CostEstimate(
            flops=int(work * 1e9), bytes_accessed=1, transcendentals=0
        ),
        name=name,
    )

    def placed(*operands):
        operands = [
            pltpu.with_memory_space_constraint(value, spec.memory_space)
            for value, spec in zip(operands, in_specs)
        ]
        result = run(*operands)
        return result if isinstance(out_shape, list) else result[0]

    return placed


def cuts(whole, parts):
    return [pl.ds(at * (whole // parts), whole // parts) for at in range(parts)]


def number(numbers_ref, at, step):
    return pl.multiple_of(numbers_ref[at, 0], step)


def start_copy(source, target, sem):
    copy = pltpu.make_async_copy(source, target, sem)
    copy.start()
    return copy


def split(rows, width):
    count, steps = rows.shape
    parts = []
    for _ in range(3):
        part = rows.astype(BF16).astype(F32)
        parts.append(part)
        rows = rows - part
    parts.append(jnp.zeros((16 - 3 * count, steps), F32))
    out = jnp.concatenate(parts, axis=0)
    if width > steps:
        out = jnp.concatenate([out, jnp.zeros((16, width - steps), F32)], axis=1)
    return out.astype(BF16)


def joined(parts, steps):
    wide = parts[:, :steps].astype(F32)
    return wide[:2] + wide[2:4] + wide[4:6]


def load_first(source, weights, starts, half):
    steps, units = source.shape
    spans = 4
    width = units // spans

    def kernel(starts_ref, source_ref, weights_ref, sent_ref, hidden_ref, *refs):
        held, following, pre, total, sems, sem = refs
        rows = pl.ds(number(starts_ref, 0, half), half)
        later = pl.ds(number(starts_ref, 2, half), half)

        def copies(at):
            span = pl.ds(pl.multiple_of(at * width, width), width)
            return span, (
                pltpu.make_async_copy(source_ref.at[:, span], pre.at[:, span], sems.at[0, at]),
                pltpu.make_async_copy(
                    weights_ref.at[rows, span], held.at[:, span], sems.at[1, at]
                ),
            )

        def start(at):
            for copy in copies(at)[1]:
                copy.start()

        for at in range(spans):
            start(at)
        copy = start_copy(weights_ref.at[later, :], following, sem)
        total[...] = jnp.zeros_like(total)

        def step(at, carry):
            span, pair = copies(at)
            for copy in pair:
                copy.wait()
            hidden = silu(pre[:, span])
            hidden_ref[pl.ds(0, steps), span] = hidden
            total[...] += lax.dot_general(
                hidden, held[:, span], NT, preferred_element_type=F32
            )
            return carry

        lax.fori_loop(0, spans, step, 0)
        sent_ref[...] = total[...].astype(BF16)
        copy.wait()

    return call(
        kernel,
        [
            in_vmem((steps, half), BF16),
            in_vmem((2 * steps, units), BF16),
            in_vmem((half, units), BF16),
            in_vmem((half, units), BF16),
            in_vmem((steps, units), BF16),
        ],
        [VMEM, HBM, HBM],
        [
            pltpu.VMEM((steps, half), F32),
            pltpu.SemaphoreType.DMA((2, spans)),
            pltpu.SemaphoreType.DMA,
        ],
        name="load_first",
    )(starts, source, weights)


def load_second(source, weights, starts, held, hidden, following):
    steps, units = source.shape
    half = held.shape[0]

    def kernel(
        starts_ref, source_ref, weights_ref, held_ref, _, out_ref, hidden_ref, block, sem
    ):
        first = number(starts_ref, following, half)
        copy = start_copy(weights_ref.at[pl.ds(first, half), :], block, sem)

        @pl.when(first >= 0)
        def _():
            total = None
            for span in cuts(units, 4):
                hidden = silu(source_ref[:, span])
                hidden_ref[pl.ds(steps, steps), span] = hidden
                term = lax.dot_general(hidden, held_ref[:, span], NT, preferred_element_type=F32)
                total = term if total is None else total + term
            out_ref[...] = total.astype(BF16)

        copy.wait()

    return call(
        kernel,
        [
            in_vmem((steps, half), BF16),
            in_vmem((2 * steps, units), BF16),
            in_vmem((half, units), BF16),
        ],
        [VMEM, VMEM, HBM, VMEM, VMEM],
        [pltpu.SemaphoreType.DMA],
        aliases={4: 1},
        name="load_second",
    )(starts, source, weights, held, hidden)


def project(hidden, rows, out_type, weights, starts, following):
    steps, units = hidden.shape
    half = rows.shape[0]

    def product(hidden_ref, rows_ref, out_ref):
        total = lax.dot_general(hidden_ref[...], rows_ref[...], NT, preferred_element_type=F32)
        out_ref[...] = total.astype(out_type)

    def loading(starts_ref, weights_ref, hidden_ref, rows_ref, out_ref, block, sem):
        start = number(starts_ref, following, half)
        copy = start_copy(weights_ref.at[pl.ds(start, half), :], block, sem)

        @pl.when(start >= 0)
        def _():
            product(hidden_ref, rows_ref, out_ref)

        copy.wait()

    out_shape = in_vmem((steps, half), out_type)
    if following is None:
        return [call(product, out_shape, [VMEM] * 2, work=2 * WORK, name="project")(hidden, rows)]
    return call(
        loading,
        [out_shape, in_vmem((half, units), BF16)],
        [VMEM, HBM, VMEM, VMEM],
        [pltpu.SemaphoreType.DMA],
        name="project",
    )(starts, weights, hidden, rows)


def lane_sums(value):
    width = value.shape[1]
    if width % 128 == 0:
        squares = value * value
        squares = sum(squares[:, at : at + 128] for at in range(0, width, 128))
        return jnp.sum(squares.T, axis=0, keepdims=True)
    ones = jnp.ones((8, value.shape[1]), F32)
    sums = lax.dot_general(
        ones, value * value, NT, precision=lax.Precision.HIGHEST, preferred_element_type=F32
    )
    return sums[:1]


def half_of(place, steps):
    return pl.ds(pl.multiple_of(place * steps, steps), steps)


def predicted_of(kept, arriving, starts, squares, packed):
    steps, width = kept.shape[0] // 2, kept.shape[1]

    def kernel(starts_ref, kept_ref, *refs):
        sent_ref, total_ref, squares_ref = refs[-3:]
        rows = []
        for at in range(2):
            part = pl.ds(at * steps, steps)
            arrived = refs[0][part, :] if len(arriving) == 1 else refs[at][...]
            total = kept_ref[part, :] + arrived.astype(F32)
            total_ref[part, :] = total
            rows.append(lane_sums(total))
        sent_ref[pl.ds(0, steps), :] = total_ref[half_of(1 - starts_ref[7, 0], steps), :].astype(BF16)
        both = jnp.concatenate(rows, axis=0)
        if squares is not None:
            both += refs[len(arriving)][...]
        squares_ref[...] = both
        if packed:
            sent_ref[pl.ds(steps, 16), :] = split(both, width)

    shapes = [
        in_vmem((steps + 16 * packed, width), BF16),
        in_vmem((2 * steps, width), F32),
        in_vmem((2, steps), F32),
    ]
    more = [] if squares is None else [squares]
    operands = [starts, kept, *arriving, *more]
    return call(kernel, shapes, [VMEM] * len(operands), name="predicted")(*operands)


def sum_of(total, arriving, starts, squares, packed, out_packed):
    steps, width = arriving.shape[0] - 16 * packed, arriving.shape[1]

    def kernel(starts_ref, total_ref, arriving_ref, *refs):
        sent_ref, out_ref = refs[-2:] if squares is None else refs[1:3]
        held = total_ref[half_of(starts_ref[7, 0], steps), :] if total.shape[0] > steps else total_ref[...]
        out = held + arriving_ref[pl.ds(0, steps), :].astype(F32)
        sent_ref[pl.ds(0, steps), :] = out.astype(BF16)
        out_ref[...] = out
        if squares is None:
            return
        both = refs[0][...]
        if packed:
            both += joined(arriving_ref[pl.ds(steps, 16), :], both.shape[1])
        refs[3][...] = both
        if out_packed:
            sent_ref[pl.ds(steps, 16), :] = split(both, width)

    shapes = [
        in_vmem((steps + 16 * out_packed, width), BF16),
        in_vmem((steps, width), F32),
    ]
    more = [] if squares is None else [squares]
    shapes += [in_vmem(value.shape, F32) for value in more]
    return call(kernel, shapes, [VMEM] * (3 + len(more)), name="sum_of")(
        starts, total, arriving, *more
    )


def kept_gradient(total, predicted, starts, cotangents, members, factor):
    steps, width = total.shape

    def kernel(starts_ref, total_ref, predicted_ref, own, other, grad_ref):
        first = starts_ref[7, 0] == 0
        weighting = jnp.where(first, own[:, :1], other[:, :1]).astype(F32) * factor
        predicted_rows = predicted_ref[half_of(starts_ref[7, 0], steps), :]
        grad_ref[...] = (weighting * (predicted_rows - total_ref[...] / members)).astype(BF16)

    operands = [starts, total, predicted, *cotangents]
    return call(
        kernel,
        in_vmem((steps, width), BF16),
        [VMEM] * len(operands),
        name="kept_gradient",
    )(*operands)


def gradient_of(total, arriving, predicted, starts, cotangents, members, factor, sums, passed):
    steps, width = total.shape
    squares, previous, packed = sums

    def kernel(starts_ref, total_ref, arriving_ref, predicted_ref, own, other, *refs):
        refs, mean_ref = list(refs[:-1]), refs[-1]
        previous_ref = refs.pop(0) if previous is not None else None
        squares_ref = refs.pop(0) if squares is not None else None
        if passed is not None:
            passed_ref = refs.pop(0)
            refs[0][pl.ds(steps, steps), :] = passed_ref[...]
        sent_ref, grad_ref, sums_ref = refs
        mean_ref[half_of(starts_ref[7, 0], steps), :] = total_ref[...] / members
        mean_ref[half_of(1 - starts_ref[7, 0], steps), :] = arriving_ref[...].astype(F32) / members
        rows = []
        for at, cotangent_ref in enumerate((own, other)):
            part = pl.ds(at * steps, steps)
            mean = mean_ref[part, :]
            weighting = cotangent_ref[:, :1].astype(F32) * factor
            grad_ref[part, :] = (weighting * (predicted_ref[part, :] - mean)).astype(BF16)
            rows.append(lane_sums(mean))
        sent_ref[pl.ds(0, steps), :] = grad_ref[half_of(1 - starts_ref[7, 0], steps), :]
        both = jnp.concatenate(rows, axis=0)
        if previous is not None:
            both += previous_ref[...]
        if squares is not None:
            both = squares_ref[...] / members - both
        sums_ref[...] = both
        if packed:
            sent_ref[pl.ds(steps, 16), :] = split(both, width)

    operands = [starts, total, arriving, predicted, *cotangents]
    operands += [value for value in (previous, squares, passed) if value is not None]
    below = 16 * packed if passed is None else steps
    return call(
        kernel,
        [
            in_vmem((steps + below, width), BF16),
            in_vmem((2 * steps, width), BF16),
            in_vmem((2, steps), F32),
        ],
        [VMEM] * len(operands),
        [pltpu.VMEM((2 * steps, width), F32)],
        name="gradient",
    )(*operands)


def in_place(kept, rest, starts, steps, offset):
    def kernel(starts_ref, kept_ref, rest_ref, out_ref):
        out_ref[half_of(starts_ref[7, 0], steps), :] = kept_ref[pl.ds(offset, steps), :]
        out_ref[half_of(1 - starts_ref[7, 0], steps), :] = rest_ref[pl.ds(0, steps), :]

    out_shape = in_vmem((2 * steps, kept.shape[1]), BF16)
    return call(kernel, out_shape, [VMEM] * 3, name="in_place")(starts, kept, rest)


def plus(first, second):
    def kernel(first_ref, second_ref, out_ref):
        out_ref[...] = first_ref[...] + second_ref[...]

    return call(kernel, in_vmem(first.shape, F32), [VMEM, VMEM], name="plus")(first, second)


def leave_to_other(first, second, before, spread, arriving_spread, steps):
    units = before.shape[1]
    packed = arriving_spread.shape[0] > 2

    def kernel(g0, rows0, g1, rows1, before_ref, spread_ref, arriving_ref, out_ref, sum_ref):
        for span in cuts(units, 4):
            total = before_ref[pl.ds(steps, steps), span]
            for grad, rows in ((g0, rows0), (g1, rows1)):
                total += jnp.dot(
                    grad[pl.ds(steps, steps), :], rows[:, span], preferred_element_type=F32
                )
            out_ref[pl.ds(0, steps), span] = total.astype(BF16)
        if packed:
            both = spread_ref[...] + joined(arriving_ref[pl.ds(steps, 16), :], steps)
        else:
            both = spread_ref[...] + arriving_ref[...]
        sum_ref[...] = both
        out_ref[pl.ds(steps, 16), :] = split(both, units)

    shapes = [in_vmem((steps + 16, units), BF16), in_vmem((2, steps), F32)]
    return call(kernel, shapes, [VMEM] * 7, name="leave_to_other")(
        *first, *second, before, spread, arriving_spread
    )


def send_block(made, at, starts_ref, block, out_ref, sems):
    half = made.shape[1]
    to = pl.ds(number(starts_ref, block, half), half)
    return start_copy(made.at[at], out_ref.at[to, :], sems.at[at])


def kept_products(kept, hidden, rows, starts):
    (steps, half), units = kept.shape, rows.shape[1]

    def kernel(starts_ref, kept_ref, h, rows_ref, term_ref, back_ref):
        part = half_of(starts_ref[7, 0], steps)
        for span in cuts(units, 4):
            term = lax.dot_general(kept_ref[...], h[part, span], TN, preferred_element_type=F32)
            term_ref[:, span] = term.astype(BF16)
            back_ref[:, span] = jnp.dot(
                kept_ref[...], rows_ref[:, span], preferred_element_type=F32
            )

    shapes = [in_vmem((half, units), BF16), in_vmem((steps, units), F32)]
    return call(kernel, shapes, [VMEM] * 4, name="kept_products")(starts, kept, hidden, rows)


def first_blocks(first, second, term, hidden, starts, blocks, features, rows, kept_back):
    half, (steps, units) = first.shape[1], kept_back.shape

    def kernel(starts_ref, g0, g1, term_ref, h, w0, w1, kept_ref, out_ref, sum_ref, made, sems):
        kept, rest = half_of(starts_ref[7, 0], steps), half_of(1 - starts_ref[7, 0], steps)
        for span in cuts(units, 4):
            total = lax.dot_general(g1[...], h[:, span], TN, preferred_element_type=F32)
            made[1, :, span] = total.astype(BF16)
        copies = [send_block(made, 1, starts_ref, blocks[1], out_ref, sems)]
        for span in cuts(units, 4):
            total = lax.dot_general(g0[rest, :], h[rest, span], TN, preferred_element_type=F32)
            made[0, :, span] = (total + term_ref[:, span].astype(F32)).astype(BF16)
        copies.append(send_block(made, 0, starts_ref, blocks[0], out_ref, sems))

        @pl.when(starts_ref[7, 0] >= 0)
        def _():
            for span in cuts(units, 4):
                for part, more in ((kept, kept_ref), (rest, None)):
                    total = jnp.dot(g1[part, :], w1[:, span], preferred_element_type=F32)
                    if more is None:
                        total += jnp.dot(g0[part, :], w0[:, span], preferred_element_type=F32)
                    else:
                        total += more[:, span]
                    sum_ref[part, span] = total

        for copy in copies:
            copy.wait()

    return call(
        kernel,
        [in_hbm((features, units), BF16), in_vmem((2 * steps, units), F32)],
        [VMEM] * 8,
        [pltpu.VMEM((2, half, units), BF16), pltpu.SemaphoreType.DMA((2,))],
        name="first_blocks",
    )(starts, first, second, term, hidden, *rows, kept_back)


def last_blocks(grads, hidden, starts, blocks, started, rows, before):
    (features, units), half = started.shape, grads[0].shape[1]
    steps = before.shape[0] // 2

    def kernel(starts_ref, g0, g1, h, w0, w1, before_ref, _, out_ref, sum_ref, made, sems):
        copies = []
        for at, grad in enumerate((g0, g1)):
            for span in cuts(units, 4):
                total = lax.dot_general(grad[...], h[:, span], TN, preferred_element_type=F32)
                made[at, :, span] = total.astype(BF16)
            copies.append(send_block(made, at, starts_ref, blocks[at], out_ref, sems))

        @pl.when(starts_ref[7, 0] >= 0)
        def _():
            own = pl.ds(0, steps)
            for span in cuts(units, 4):
                total = jnp.dot(g0[own, :], w0[:, span], preferred_element_type=F32)
                total += jnp.dot(g1[own, :], w1[:, span], preferred_element_type=F32)
                sum_ref[:, span] = total + before_ref[own, span]

        for copy in copies:
            copy.wait()

    return call(
        kernel,
        [in_hbm((features, units), BF16), in_vmem((steps, units), F32)],
        [VMEM] * 7 + [HBM],
        [pltpu.VMEM((2, half, units), BF16), pltpu.SemaphoreType.DMA((2,))],
        aliases={7: 0},
        name="last_blocks",
    )(starts, *grads, hidden, *rows, before, started)


def slope_of(pre_act):
    def kernel(pre, slope_ref):
        for span in cuts(pre_act.shape[1], 4):
            wide = pre[:, span].astype(F32)
            gate = sigmoid(wide)
            slope_ref[:, span] = gate * (1.0 + wide * (1.0 - gate))

    return call(kernel, in_vmem(pre_act.shape, F32), [VMEM], name="slope_of")(pre_act)


def last_grads(before, arrived, slope, spread, model_width):
    steps, units = before.shape
    lanes = -(-steps // 128) * 128

    def kernel(
        before_ref, arrived_ref, slope, spread_ref, act_ref, reward_ref, act, reward, sems
    ):
        others = joined(arrived_ref[pl.ds(steps, 16), pl.ds(0, lanes)], steps)
        reward[...] = (spread_ref[...][:1] + others[1:]) / model_width
        copies = [start_copy(reward, reward_ref, sems.at[4])]
        for at, span in enumerate(cuts(units, 4)):
            total = before_ref[:, span] + arrived_ref[pl.ds(0, steps), span].astype(F32)
            act[:, span] = (total * slope[:, span]).astype(BF16)
            copies.append(start_copy(act.at[:, span], act_ref.at[:, span], sems.at[at]))
        for copy in copies:
            copy.wait()

    return call(
        kernel,
        [in_hbm((steps, units), BF16), in_hbm((1, steps), F32)],
        [VMEM] * 4,
        [
            pltpu.VMEM((steps, units), BF16),
            pltpu.VMEM((1, steps), F32),
            pltpu.SemaphoreType.DMA((5,)),
        ],
        name="last_grads",
    )(before, arrived, slope, spread)


class Order:
    def __init__(self):
        self.last = None

    def __call__(self, step, *values):
        if self.last is not None:
            values, _ = lax.optimization_barrier((values, self.last))
        result = step(*values)
        self.last = jax.tree.leaves(result)[0]
        return result


class Piece:
    def __init__(self, order, starts, last, previous):
        self.order, self.starts = order, starts
        self.last, self.previous = last, previous
        self.tensor = lax.axis_index("tensor")
        self.arriving = []

    def leave(self, sent):
        self.arriving.append(swap(sent, "tensor", shares(lax.axis_size("tensor"))[-1]))

    def scatter_rest(self):
        def add(total, arriving):
            return total + arriving.astype(F32)

        for distance in reversed(shares(lax.axis_size("tensor"))[:-1]):
            half = self.total.shape[1] // 2
            high = (self.tensor // distance) % 2
            total = self.order(add, self.total, jnp.concatenate(self.arriving))
            sent = lax.dynamic_slice_in_dim(total, (1 - high) * half, half, 1)
            self.total = lax.dynamic_slice_in_dim(total, high * half, half, 1)
            self.arriving = [swap(sent.astype(BF16), "tensor", distance)]

    def predict(self):
        steps, width = self.total.shape[0] // 2, self.total.shape[1]
        self.packed = self.last and width >= steps
        before = None if self.previous is None else self.previous.squares
        sent, self.predicted, self.squares = self.order(
            lambda kept, *arriving: predicted_of(
                kept, arriving, self.starts, before, self.packed
            ),
            self.total,
            *self.arriving,
        )
        self.sum = self.predicted
        near, *self.far = shares(lax.axis_size("ensemble"))
        self.arriving = swap(sent, "ensemble", near)
        self.exchange_squares(near)

    def exchange_squares(self, distance):
        self.squares_arriving = None
        if self.last and not self.packed:
            self.squares_arriving = swap(self.squares, "ensemble", distance)

    def ensemble_steps(self):
        packed = self.packed
        for distance in self.far + [None]:
            out_packed = self.packed and distance is not None
            before = self.squares if self.last else None
            sent, self.sum, *squares = self.order(
                lambda total, arriving: sum_of(
                    total, arriving, self.starts, before, packed, out_packed
                ),
                self.sum,
                self.arriving,
            )
            if self.last:
                self.squares = squares[0]
            if self.squares_arriving is not None:
                self.squares = self.order(plus, self.squares, self.squares_arriving)
            if distance is not None:
                self.arriving = swap(sent, "ensemble", distance)
                self.exchange_squares(distance)
                yield
            else:
                self.arriving = swap(sent, "ensemble", 1)

    def gather(self, share):
        def join(share, other, distance):
            high = (self.tensor // distance) % 2
            first = jnp.where(high == 0, share, other)
            second = jnp.where(high == 0, other, share)
            return jnp.concatenate([first, second], axis=1)

        *near, far = shares(lax.axis_size("tensor"))
        for distance in near:
            other = swap(share, "tensor", distance)
            share = self.order(functools.partial(join, distance=distance), share, other)
        return share, swap(share, "tensor", far)

    def early_gradient(self, cotangents, members, factor):
        return self.order(
            lambda total: kept_gradient(
                total, self.predicted, self.starts, cotangents, members, factor
            ),
            self.sum,
        )

    def gradient(self, cotangents, members, factor, passed=None):
        *near, far = shares(lax.axis_size("tensor"))
        packed = self.last and not near and self.sum.shape[1] >= self.sum.shape[0]
        sums = (
            self.squares if self.last else None,
            None if self.previous is None else self.previous.sums,
            packed,
        )
        sent, self.share, self.sums = self.order(
            lambda total, arriving: gradient_of(
                total,
                arriving,
                self.predicted,
                self.starts,
                cotangents,
                members,
                factor,
                sums,
                passed,
            ),
            self.sum,
            self.arriving,
        )
        self.rest = self.gather(sent)
        self.other_sums = self.rest[1]
        if self.last and not packed:
            for distance in near:
                self.sums = self.order(plus, self.sums, swap(self.sums, "tensor", distance))
            self.other_sums = swap(self.sums, "tensor", far)
        if near:
            self.share = self.together(0)

    def together(self, which):
        steps = self.sum.shape[0]
        return self.order(
            lambda kept, rest: in_place(kept, rest, self.starts, steps, self.offset),
            self.kept[which],
            self.rest[which],
        )


def body(pre_act, weights, cotangent):
    pre_act, weights = pre_act[:, 0, :], weights[0]
    steps, features = pre_act.shape[0], weights.shape[0]
    members = lax.axis_size("ensemble")
    model_width = features * lax.axis_size("seq")
    factor = 2.0 / (members * model_width)
    half = features // (2 * PIECES)
    far = shares(lax.axis_size("tensor"))[-1]
    high = (lax.axis_index("tensor") // far) % 2
    starts = []
    for piece in range(PIECES):
        starts += [(2 * piece + 1 - high) * half, (2 * piece + high) * half]
    assert len(starts) < 8
    starts += [0] * (7 - len(starts)) + [lax.axis_index("ensemble") % 2]
    starts = jnp.broadcast_to(jnp.stack(starts).astype(jnp.int32)[:, None], (8, 128))

    pre_other = swap(pre_act, "seq", 1)
    pre_act, starts = lax.optimization_barrier((pre_act, starts))
    order = Order()
    pieces = []
    for at in range(PIECES):
        previous = pieces[-1] if pieces else None
        pieces.append(Piece(order, starts, at == PIECES - 1, previous))
    blocks = [None] * (2 * PIECES)
    sent, hidden, blocks[0], blocks[2], pre_act = order(
        lambda p: load_first(p, weights, starts, half), pre_act
    )
    pieces[0].leave(sent)
    sent, hidden, blocks[1] = order(
        lambda p, h: load_second(p, weights, starts, blocks[0], h, 1), pre_other, hidden
    )
    pieces[0].leave(sent)

    def products(at, following):
        out = order(
            lambda rows: project(
                hidden, rows, F32 if at % 2 else BF16, weights, starts, following
            ),
            blocks[at],
        )
        if following is not None:
            blocks[following] = out[1]
        return out[0]

    a, b = pieces
    b.leave(products(2, 3))
    a.total = products(1, None)
    a.scatter_rest()
    a.predict()
    b.total = products(3, None)
    cot_other = swap(order(lambda c: c, cotangent), "seq", 1)
    b.scatter_rest()
    b.predict()
    a_steps, b_steps = a.ensemble_steps(), b.ensemble_steps()
    next(a_steps)
    for _ in b.far:
        next(b_steps)
        slope = order(slope_of, pre_act)
        next(a_steps, None)
    cotangents = [
        order(lambda c: jnp.broadcast_to(c[:, None], (steps, 128)), value)
        for value in (cotangent, cot_other)
    ]
    kept = a.early_gradient(cotangents, members, factor)
    a.kept, a.offset = a.gather(kept), 0
    rows_early, rows_late = [blocks[1], blocks[3]], [blocks[0], blocks[2]]
    next(b_steps, None)
    term, kept_back = order(
        lambda g: kept_products(g, hidden, blocks[1], starts), a.kept[0]
    )
    kept = b.early_gradient(cotangents, members, factor)
    a.kept = a.kept[0], order(lambda x: x, a.kept[1])
    a.gradient(cotangents, members, factor, kept)
    b.kept, b.offset = a.rest, steps
    b.gradient(cotangents, members, factor)
    weight_grads, before = order(
        lambda x, y: first_blocks(
            x, y, term, hidden, starts, [1, 3], features, rows_early, kept_back
        ),
        a.share,
        b.share,
    )
    a_other = a.together(1)
    b_other = b.together(1)
    leaving, spread = order(
        lambda x, y, z: leave_to_other(
            (x, blocks[0]), (y, blocks[2]), before, b.sums, z, steps
        ),
        a_other,
        b_other,
        b.other_sums,
    )
    arrived = swap(leaving, "seq", 1)
    weight_grads, before = order(
        lambda x, y, s: last_blocks([x, y], hidden, starts, [0, 2], s, rows_late, before),
        a_other,
        b_other,
        weight_grads,
    )
    act_grads, reward = order(
        lambda g, s: last_grads(g, s, slope, spread, model_width), before, arrived
    )
    return (weight_grads[None], act_grads[:, None, :], reward[0])


def solution(mesh):
    placed = (
        P(("groups", "seq"), "ensemble", "tensor"),
        P("ensemble", "seq", "tensor"),
        P(("groups", "seq")),
    )
    return jax.shard_map(
        body,
        mesh=mesh,
        in_specs=placed,
        out_specs=(
            P(("groups", "ensemble"), "seq", "tensor"),
            P(("groups", "seq"), "ensemble", "tensor"),
            P(("groups", "seq")),
        ),
        check_vma=False,
    )
```

```python
import functools

import jax
import jax.numpy as jnp
from jax import lax
from jax.experimental import pallas as pl
from jax.experimental.pallas import tpu as pltpu
from jax.sharding import PartitionSpec as P

F32, BF16 = jnp.float32, jnp.bfloat16
NT = (((1,), (1,)), ((), ()))
TN = (((0,), (0,)), ((), ()))
PIECES = 2
WORK = 0.4
VMEM_LIMIT = 16 * 2**20


def swap(value, axis, distance):
    size = lax.axis_size(axis)
    return lax.ppermute(value, axis, [(i, i ^ distance) for i in range(size)])


def shares(size):
    return [1 << bit for bit in range(size.bit_length() - 1)]


def sigmoid(wide):
    return jax.nn.sigmoid(wide)


def silu(value):
    wide = value.astype(F32)
    return (wide * sigmoid(wide)).astype(BF16)


VMEM = pl.BlockSpec(memory_space=pltpu.VMEM)
HBM = pl.BlockSpec(memory_space=pltpu.HBM)


def in_vmem(shape, dtype):
    return pltpu.VMEM(shape, dtype)


def in_hbm(shape, dtype):
    return pltpu.HBM(shape, dtype)


def call(kernel, out_shape, in_specs, scratch=(), aliases=None, work=WORK, name=None):
    outs = out_shape if isinstance(out_shape, list) else [out_shape]
    out_specs = [pl.BlockSpec(memory_space=out.memory_space) for out in outs]
    run = pl.pallas_call(
        kernel,
        out_shape=outs,
        in_specs=in_specs,
        out_specs=out_specs,
        scratch_shapes=list(scratch),
        input_output_aliases=aliases or {},
        compiler_params=pltpu.CompilerParams(vmem_limit_bytes=VMEM_LIMIT),
        cost_estimate=pl.CostEstimate(
            flops=int(work * 1e9), bytes_accessed=1, transcendentals=0
        ),
        name=name,
    )

    def placed(*operands):
        operands = [
            pltpu.with_memory_space_constraint(value, spec.memory_space)
            for value, spec in zip(operands, in_specs)
        ]
        result = run(*operands)
        return result if isinstance(out_shape, list) else result[0]

    return placed


def cuts(whole, parts):
    return [pl.ds(at * (whole // parts), whole // parts) for at in range(parts)]


def number(numbers_ref, at, step):
    return pl.multiple_of(numbers_ref[at, 0], step)


def start_copy(source, target, sem):
    copy = pltpu.make_async_copy(source, target, sem)
    copy.start()
    return copy


def split(rows, width):
    count, steps = rows.shape
    parts = []
    for _ in range(3):
        part = rows.astype(BF16).astype(F32)
        parts.append(part)
        rows = rows - part
    parts.append(jnp.zeros((16 - 3 * count, steps), F32))
    out = jnp.concatenate(parts, axis=0)
    if width > steps:
        out = jnp.concatenate([out, jnp.zeros((16, width - steps), F32)], axis=1)
    return out.astype(BF16)


def joined(parts, steps):
    wide = parts[:, :steps].astype(F32)
    return wide[:2] + wide[2:4] + wide[4:6]


def load_first(source, weights, starts, half):
    steps, units = source.shape
    spans = 4
    width = units // spans

    def kernel(starts_ref, source_ref, weights_ref, sent_ref, hidden_ref, *refs):
        held, following, pre, total, sems, sem = refs
        rows = pl.ds(number(starts_ref, 0, half), half)
        later = pl.ds(number(starts_ref, 2, half), half)

        def copies(at):
            span = pl.ds(pl.multiple_of(at * width, width), width)
            return span, (
                pltpu.make_async_copy(source_ref.at[:, span], pre.at[:, span], sems.at[0, at]),
                pltpu.make_async_copy(
                    weights_ref.at[rows, span], held.at[:, span], sems.at[1, at]
                ),
            )

        def start(at):
            for copy in copies(at)[1]:
                copy.start()

        for at in range(spans):
            start(at)
        copy = start_copy(weights_ref.at[later, :], following, sem)
        total[...] = jnp.zeros_like(total)

        def step(at, carry):
            span, pair = copies(at)
            for copy in pair:
                copy.wait()
            hidden = silu(pre[:, span])
            hidden_ref[pl.ds(0, steps), span] = hidden
            total[...] += lax.dot_general(
                hidden, held[:, span], NT, preferred_element_type=F32
            )
            return carry

        lax.fori_loop(0, spans, step, 0)
        sent_ref[...] = total[...].astype(BF16)
        copy.wait()

    return call(
        kernel,
        [
            in_vmem((steps, half), BF16),
            in_vmem((2 * steps, units), BF16),
            in_vmem((half, units), BF16),
            in_vmem((half, units), BF16),
            in_vmem((steps, units), BF16),
        ],
        [VMEM, HBM, HBM],
        [
            pltpu.VMEM((steps, half), F32),
            pltpu.SemaphoreType.DMA((2, spans)),
            pltpu.SemaphoreType.DMA,
        ],
        name="load_first",
    )(starts, source, weights)


def load_second(source, weights, starts, held, hidden, following):
    steps, units = source.shape
    half = held.shape[0]

    def kernel(
        starts_ref, source_ref, weights_ref, held_ref, _, out_ref, hidden_ref, block, sem
    ):
        first = number(starts_ref, following, half)
        copy = start_copy(weights_ref.at[pl.ds(first, half), :], block, sem)

        @pl.when(first >= 0)
        def _():
            total = None
            for span in cuts(units, 4):
                hidden = silu(source_ref[:, span])
                hidden_ref[pl.ds(steps, steps), span] = hidden
                term = lax.dot_general(hidden, held_ref[:, span], NT, preferred_element_type=F32)
                total = term if total is None else total + term
            out_ref[...] = total.astype(BF16)

        copy.wait()

    return call(
        kernel,
        [
            in_vmem((steps, half), BF16),
            in_vmem((2 * steps, units), BF16),
            in_vmem((half, units), BF16),
        ],
        [VMEM, VMEM, HBM, VMEM, VMEM],
        [pltpu.SemaphoreType.DMA],
        aliases={4: 1},
        name="load_second",
    )(starts, source, weights, held, hidden)


def project(hidden, rows, out_type, weights, starts, following):
    steps, units = hidden.shape
    half = rows.shape[0]

    def product(hidden_ref, rows_ref, out_ref):
        total = lax.dot_general(hidden_ref[...], rows_ref[...], NT, preferred_element_type=F32)
        out_ref[...] = total.astype(out_type)

    def loading(starts_ref, weights_ref, hidden_ref, rows_ref, out_ref, block, sem):
        start = number(starts_ref, following, half)
        copy = start_copy(weights_ref.at[pl.ds(start, half), :], block, sem)

        @pl.when(start >= 0)
        def _():
            product(hidden_ref, rows_ref, out_ref)

        copy.wait()

    out_shape = in_vmem((steps, half), out_type)
    if following is None:
        return [call(product, out_shape, [VMEM] * 2, work=2 * WORK, name="project")(hidden, rows)]
    return call(
        loading,
        [out_shape, in_vmem((half, units), BF16)],
        [VMEM, HBM, VMEM, VMEM],
        [pltpu.SemaphoreType.DMA],
        name="project",
    )(starts, weights, hidden, rows)


def lane_sums(value):
    width = value.shape[1]
    if width % 128 == 0:
        squares = value * value
        squares = sum(squares[:, at : at + 128] for at in range(0, width, 128))
        return jnp.sum(squares.T, axis=0, keepdims=True)
    ones = jnp.ones((8, value.shape[1]), F32)
    sums = lax.dot_general(
        ones, value * value, NT, precision=lax.Precision.HIGHEST, preferred_element_type=F32
    )
    return sums[:1]


def half_of(place, steps):
    return pl.ds(pl.multiple_of(place * steps, steps), steps)


def predicted_of(kept, arriving, starts, squares, packed):
    steps, width = kept.shape[0] // 2, kept.shape[1]

    def kernel(starts_ref, kept_ref, *refs):
        sent_ref, total_ref, squares_ref = refs[-3:]
        rows = []
        for at in range(2):
            part = pl.ds(at * steps, steps)
            arrived = refs[0][part, :] if len(arriving) == 1 else refs[at][...]
            total = kept_ref[part, :] + arrived.astype(F32)
            total_ref[part, :] = total
            rows.append(lane_sums(total))
        sent_ref[pl.ds(0, steps), :] = total_ref[half_of(1 - starts_ref[7, 0], steps), :].astype(BF16)
        both = jnp.concatenate(rows, axis=0)
        if squares is not None:
            both += refs[len(arriving)][...]
        squares_ref[...] = both
        if packed:
            sent_ref[pl.ds(steps, 16), :] = split(both, width)

    shapes = [
        in_vmem((steps + 16 * packed, width), BF16),
        in_vmem((2 * steps, width), F32),
        in_vmem((2, steps), F32),
    ]
    more = [] if squares is None else [squares]
    operands = [starts, kept, *arriving, *more]
    return call(kernel, shapes, [VMEM] * len(operands), name="predicted")(*operands)


def sum_of(total, arriving, starts, squares, packed, out_packed):
    steps, width = arriving.shape[0] - 16 * packed, arriving.shape[1]

    def kernel(starts_ref, total_ref, arriving_ref, *refs):
        sent_ref, out_ref = refs[-2:] if squares is None else refs[1:3]
        held = total_ref[half_of(starts_ref[7, 0], steps), :] if total.shape[0] > steps else total_ref[...]
        out = held + arriving_ref[pl.ds(0, steps), :].astype(F32)
        sent_ref[pl.ds(0, steps), :] = out.astype(BF16)
        out_ref[...] = out
        if squares is None:
            return
        both = refs[0][...]
        if packed:
            both += joined(arriving_ref[pl.ds(steps, 16), :], both.shape[1])
        refs[3][...] = both
        if out_packed:
            sent_ref[pl.ds(steps, 16), :] = split(both, width)

    shapes = [
        in_vmem((steps + 16 * out_packed, width), BF16),
        in_vmem((steps, width), F32),
    ]
    more = [] if squares is None else [squares]
    shapes += [in_vmem(value.shape, F32) for value in more]
    return call(kernel, shapes, [VMEM] * (3 + len(more)), name="sum_of")(
        starts, total, arriving, *more
    )


def kept_gradient(total, predicted, starts, cotangents, members, factor):
    steps, width = total.shape

    def kernel(starts_ref, total_ref, predicted_ref, own, other, grad_ref):
        first = starts_ref[7, 0] == 0
        weighting = jnp.where(first, own[:, :1], other[:, :1]).astype(F32) * factor
        predicted_rows = predicted_ref[half_of(starts_ref[7, 0], steps), :]
        grad_ref[...] = (weighting * (predicted_rows - total_ref[...] / members)).astype(BF16)

    operands = [starts, total, predicted, *cotangents]
    return call(
        kernel,
        in_vmem((steps, width), BF16),
        [VMEM] * len(operands),
        name="kept_gradient",
    )(*operands)


def gradient_of(total, arriving, predicted, starts, cotangents, members, factor, sums, passed):
    steps, width = total.shape
    squares, previous, packed = sums

    def kernel(starts_ref, total_ref, arriving_ref, predicted_ref, own, other, *refs):
        refs, mean_ref = list(refs[:-1]), refs[-1]
        previous_ref = refs.pop(0) if previous is not None else None
        squares_ref = refs.pop(0) if squares is not None else None
        if passed is not None:
            passed_ref = refs.pop(0)
            refs[0][pl.ds(steps, steps), :] = passed_ref[...]
        sent_ref, grad_ref, sums_ref = refs
        mean_ref[half_of(starts_ref[7, 0], steps), :] = total_ref[...] / members
        mean_ref[half_of(1 - starts_ref[7, 0], steps), :] = arriving_ref[...].astype(F32) / members
        rows = []
        for at, cotangent_ref in enumerate((own, other)):
            part = pl.ds(at * steps, steps)
            mean = mean_ref[part, :]
            weighting = cotangent_ref[:, :1].astype(F32) * factor
            grad_ref[part, :] = (weighting * (predicted_ref[part, :] - mean)).astype(BF16)
            rows.append(lane_sums(mean))
        sent_ref[pl.ds(0, steps), :] = grad_ref[half_of(1 - starts_ref[7, 0], steps), :]
        both = jnp.concatenate(rows, axis=0)
        if previous is not None:
            both += previous_ref[...]
        if squares is not None:
            both = squares_ref[...] / members - both
        sums_ref[...] = both
        if packed:
            sent_ref[pl.ds(steps, 16), :] = split(both, width)

    operands = [starts, total, arriving, predicted, *cotangents]
    operands += [value for value in (previous, squares, passed) if value is not None]
    below = 16 * packed if passed is None else steps
    return call(
        kernel,
        [
            in_vmem((steps + below, width), BF16),
            in_vmem((2 * steps, width), BF16),
            in_vmem((2, steps), F32),
        ],
        [VMEM] * len(operands),
        [pltpu.VMEM((2 * steps, width), F32)],
        name="gradient",
    )(*operands)


def in_place(kept, rest, starts, steps, offset):
    def kernel(starts_ref, kept_ref, rest_ref, out_ref):
        out_ref[half_of(starts_ref[7, 0], steps), :] = kept_ref[pl.ds(offset, steps), :]
        out_ref[half_of(1 - starts_ref[7, 0], steps), :] = rest_ref[pl.ds(0, steps), :]

    out_shape = in_vmem((2 * steps, kept.shape[1]), BF16)
    return call(kernel, out_shape, [VMEM] * 3, name="in_place")(starts, kept, rest)


def plus(first, second):
    def kernel(first_ref, second_ref, out_ref):
        out_ref[...] = first_ref[...] + second_ref[...]

    return call(kernel, in_vmem(first.shape, F32), [VMEM, VMEM], name="plus")(first, second)


def leave_to_other(first, second, before, spread, arriving_spread, steps):
    units = before.shape[1]
    packed = arriving_spread.shape[0] > 2

    def kernel(g0, rows0, g1, rows1, before_ref, spread_ref, arriving_ref, out_ref, sum_ref):
        for span in cuts(units, 4):
            total = before_ref[pl.ds(steps, steps), span]
            for grad, rows in ((g0, rows0), (g1, rows1)):
                total += jnp.dot(
                    grad[pl.ds(steps, steps), :], rows[:, span], preferred_element_type=F32
                )
            out_ref[pl.ds(0, steps), span] = total.astype(BF16)
        if packed:
            both = spread_ref[...] + joined(arriving_ref[pl.ds(steps, 16), :], steps)
        else:
            both = spread_ref[...] + arriving_ref[...]
        sum_ref[...] = both
        out_ref[pl.ds(steps, 16), :] = split(both, units)

    shapes = [in_vmem((steps + 16, units), BF16), in_vmem((2, steps), F32)]
    return call(kernel, shapes, [VMEM] * 7, name="leave_to_other")(
        *first, *second, before, spread, arriving_spread
    )


def send_block(made, at, starts_ref, block, out_ref, sems):
    half = made.shape[1]
    to = pl.ds(number(starts_ref, block, half), half)
    return start_copy(made.at[at], out_ref.at[to, :], sems.at[at])


def kept_products(kept, hidden, rows, starts):
    (steps, half), units = kept.shape, rows.shape[1]

    def kernel(starts_ref, kept_ref, h, rows_ref, term_ref, back_ref):
        part = half_of(starts_ref[7, 0], steps)
        for span in cuts(units, 4):
            term = lax.dot_general(kept_ref[...], h[part, span], TN, preferred_element_type=F32)
            term_ref[:, span] = term.astype(BF16)
            back_ref[:, span] = jnp.dot(
                kept_ref[...], rows_ref[:, span], preferred_element_type=F32
            )

    shapes = [in_vmem((half, units), BF16), in_vmem((steps, units), F32)]
    return call(kernel, shapes, [VMEM] * 4, name="kept_products")(starts, kept, hidden, rows)


def first_blocks(first, second, term, hidden, starts, blocks, features, rows, kept_back):
    half, (steps, units) = first.shape[1], kept_back.shape

    def kernel(starts_ref, g0, g1, term_ref, h, w0, w1, kept_ref, out_ref, sum_ref, made, sems):
        kept, rest = half_of(starts_ref[7, 0], steps), half_of(1 - starts_ref[7, 0], steps)
        for span in cuts(units, 4):
            total = lax.dot_general(g1[...], h[:, span], TN, preferred_element_type=F32)
            made[1, :, span] = total.astype(BF16)
        copies = [send_block(made, 1, starts_ref, blocks[1], out_ref, sems)]
        for span in cuts(units, 4):
            total = lax.dot_general(g0[rest, :], h[rest, span], TN, preferred_element_type=F32)
            made[0, :, span] = (total + term_ref[:, span].astype(F32)).astype(BF16)
        copies.append(send_block(made, 0, starts_ref, blocks[0], out_ref, sems))

        @pl.when(starts_ref[7, 0] >= 0)
        def _():
            for span in cuts(units, 4):
                for part, more in ((kept, kept_ref), (rest, None)):
                    total = jnp.dot(g1[part, :], w1[:, span], preferred_element_type=F32)
                    if more is None:
                        total += jnp.dot(g0[part, :], w0[:, span], preferred_element_type=F32)
                    else:
                        total += more[:, span]
                    sum_ref[part, span] = total

        for copy in copies:
            copy.wait()

    return call(
        kernel,
        [in_hbm((features, units), BF16), in_vmem((2 * steps, units), F32)],
        [VMEM] * 8,
        [pltpu.VMEM((2, half, units), BF16), pltpu.SemaphoreType.DMA((2,))],
        name="first_blocks",
    )(starts, first, second, term, hidden, *rows, kept_back)


def last_blocks(grads, hidden, starts, blocks, started, rows, before):
    (features, units), half = started.shape, grads[0].shape[1]
    steps = before.shape[0] // 2

    def kernel(starts_ref, g0, g1, h, w0, w1, before_ref, _, out_ref, sum_ref, made, sems):
        copies = []
        for at, grad in enumerate((g0, g1)):
            for span in cuts(units, 4):
                total = lax.dot_general(grad[...], h[:, span], TN, preferred_element_type=F32)
                made[at, :, span] = total.astype(BF16)
            copies.append(send_block(made, at, starts_ref, blocks[at], out_ref, sems))

        @pl.when(starts_ref[7, 0] >= 0)
        def _():
            own = pl.ds(0, steps)
            for span in cuts(units, 4):
                total = jnp.dot(g0[own, :], w0[:, span], preferred_element_type=F32)
                total += jnp.dot(g1[own, :], w1[:, span], preferred_element_type=F32)
                sum_ref[:, span] = total + before_ref[own, span]

        for copy in copies:
            copy.wait()

    return call(
        kernel,
        [in_hbm((features, units), BF16), in_vmem((steps, units), F32)],
        [VMEM] * 7 + [HBM],
        [pltpu.VMEM((2, half, units), BF16), pltpu.SemaphoreType.DMA((2,))],
        aliases={7: 0},
        name="last_blocks",
    )(starts, *grads, hidden, *rows, before, started)


def slope_of(pre_act):
    def kernel(pre, slope_ref):
        for span in cuts(pre_act.shape[1], 4):
            wide = pre[:, span].astype(F32)
            gate = sigmoid(wide)
            slope_ref[:, span] = gate * (1.0 + wide * (1.0 - gate))

    return call(kernel, in_vmem(pre_act.shape, F32), [VMEM], name="slope_of")(pre_act)


def last_grads(before, arrived, slope, spread, model_width):
    steps, units = before.shape
    lanes = -(-steps // 128) * 128

    def kernel(
        before_ref, arrived_ref, slope, spread_ref, act_ref, reward_ref, act, reward, sems
    ):
        others = joined(arrived_ref[pl.ds(steps, 16), pl.ds(0, lanes)], steps)
        reward[...] = (spread_ref[...][:1] + others[1:]) / model_width
        copies = [start_copy(reward, reward_ref, sems.at[4])]
        for at, span in enumerate(cuts(units, 4)):
            total = before_ref[:, span] + arrived_ref[pl.ds(0, steps), span].astype(F32)
            act[:, span] = (total * slope[:, span]).astype(BF16)
            copies.append(start_copy(act.at[:, span], act_ref.at[:, span], sems.at[at]))
        for copy in copies:
            copy.wait()

    return call(
        kernel,
        [in_hbm((steps, units), BF16), in_hbm((1, steps), F32)],
        [VMEM] * 4,
        [
            pltpu.VMEM((steps, units), BF16),
            pltpu.VMEM((1, steps), F32),
            pltpu.SemaphoreType.DMA((5,)),
        ],
        name="last_grads",
    )(before, arrived, slope, spread)


class Order:
    def __init__(self):
        self.last = None

    def __call__(self, step, *values):
        if self.last is not None:
            values, _ = lax.optimization_barrier((values, self.last))
        result = step(*values)
        self.last = jax.tree.leaves(result)[0]
        return result


class Piece:
    def __init__(self, order, starts, last, previous):
        self.order, self.starts = order, starts
        self.last, self.previous = last, previous
        self.tensor = lax.axis_index("tensor")
        self.arriving = []

    def leave(self, sent):
        self.arriving.append(swap(sent, "tensor", shares(lax.axis_size("tensor"))[-1]))

    def scatter_rest(self):
        def add(total, arriving):
            return total + arriving.astype(F32)

        for distance in reversed(shares(lax.axis_size("tensor"))[:-1]):
            half = self.total.shape[1] // 2
            high = (self.tensor // distance) % 2
            total = self.order(add, self.total, jnp.concatenate(self.arriving))
            sent = lax.dynamic_slice_in_dim(total, (1 - high) * half, half, 1)
            self.total = lax.dynamic_slice_in_dim(total, high * half, half, 1)
            self.arriving = [swap(sent.astype(BF16), "tensor", distance)]

    def predict(self):
        steps, width = self.total.shape[0] // 2, self.total.shape[1]
        self.packed = self.last and width >= steps
        before = None if self.previous is None else self.previous.squares
        sent, self.predicted, self.squares = self.order(
            lambda kept, *arriving: predicted_of(
                kept, arriving, self.starts, before, self.packed
            ),
            self.total,
            *self.arriving,
        )
        self.sum = self.predicted
        near, *self.far = shares(lax.axis_size("ensemble"))
        self.arriving = swap(sent, "ensemble", near)
        self.exchange_squares(near)

    def exchange_squares(self, distance):
        self.squares_arriving = None
        if self.last and not self.packed:
            self.squares_arriving = swap(self.squares, "ensemble", distance)

    def ensemble_steps(self):
        packed = self.packed
        for distance in self.far + [None]:
            out_packed = self.packed and distance is not None
            before = self.squares if self.last else None
            sent, self.sum, *squares = self.order(
                lambda total, arriving: sum_of(
                    total, arriving, self.starts, before, packed, out_packed
                ),
                self.sum,
                self.arriving,
            )
            if self.last:
                self.squares = squares[0]
            if self.squares_arriving is not None:
                self.squares = self.order(plus, self.squares, self.squares_arriving)
            if distance is not None:
                self.arriving = swap(sent, "ensemble", distance)
                self.exchange_squares(distance)
                yield
            else:
                self.arriving = swap(sent, "ensemble", 1)

    def gather(self, share):
        def join(share, other, distance):
            high = (self.tensor // distance) % 2
            first = jnp.where(high == 0, share, other)
            second = jnp.where(high == 0, other, share)
            return jnp.concatenate([first, second], axis=1)

        *near, far = shares(lax.axis_size("tensor"))
        for distance in near:
            other = swap(share, "tensor", distance)
            share = self.order(functools.partial(join, distance=distance), share, other)
        return share, swap(share, "tensor", far)

    def early_gradient(self, cotangents, members, factor):
        return self.order(
            lambda total: kept_gradient(
                total, self.predicted, self.starts, cotangents, members, factor
            ),
            self.sum,
        )

    def gradient(self, cotangents, members, factor, passed=None):
        *near, far = shares(lax.axis_size("tensor"))
        packed = self.last and not near and self.sum.shape[1] >= self.sum.shape[0]
        sums = (
            self.squares if self.last else None,
            None if self.previous is None else self.previous.sums,
            packed,
        )
        sent, self.share, self.sums = self.order(
            lambda total, arriving: gradient_of(
                total,
                arriving,
                self.predicted,
                self.starts,
                cotangents,
                members,
                factor,
                sums,
                passed,
            ),
            self.sum,
            self.arriving,
        )
        self.rest = self.gather(sent)
        self.other_sums = self.rest[1]
        if self.last and not packed:
            for distance in near:
                self.sums = self.order(plus, self.sums, swap(self.sums, "tensor", distance))
            self.other_sums = swap(self.sums, "tensor", far)
        if near:
            self.share = self.together(0)

    def together(self, which):
        steps = self.sum.shape[0]
        return self.order(
            lambda kept, rest: in_place(kept, rest, self.starts, steps, self.offset),
            self.kept[which],
            self.rest[which],
        )


def body(pre_act, weights, cotangent):
    pre_act, weights = pre_act[:, 0, :], weights[0]
    steps, features = pre_act.shape[0], weights.shape[0]
    members = lax.axis_size("ensemble")
    model_width = features * lax.axis_size("seq")
    factor = 2.0 / (members * model_width)
    half = features // (2 * PIECES)
    far = shares(lax.axis_size("tensor"))[-1]
    high = (lax.axis_index("tensor") // far) % 2
    starts = []
    for piece in range(PIECES):
        starts += [(2 * piece + 1 - high) * half, (2 * piece + high) * half]
    assert len(starts) < 8
    starts += [0] * (7 - len(starts)) + [lax.axis_index("ensemble") % 2]
    row = lax.broadcasted_iota(jnp.int32, (8, 128), 0)
    starts = sum(jnp.where(row == at, value, 0) for at, value in enumerate(starts))

    pre_other = swap(pre_act, "seq", 1)
    pre_act, starts = lax.optimization_barrier((pre_act, starts))
    order = Order()
    pieces = []
    for at in range(PIECES):
        previous = pieces[-1] if pieces else None
        pieces.append(Piece(order, starts, at == PIECES - 1, previous))
    blocks = [None] * (2 * PIECES)
    sent, hidden, blocks[0], blocks[2], pre_act = order(
        lambda p: load_first(p, weights, starts, half), pre_act
    )
    pieces[0].leave(sent)
    sent, hidden, blocks[1] = order(
        lambda p, h: load_second(p, weights, starts, blocks[0], h, 1), pre_other, hidden
    )
    pieces[0].leave(sent)

    def products(at, following):
        out = order(
            lambda rows: project(
                hidden, rows, F32 if at % 2 else BF16, weights, starts, following
            ),
            blocks[at],
        )
        if following is not None:
            blocks[following] = out[1]
        return out[0]

    a, b = pieces
    b.leave(products(2, 3))
    a.total = products(1, None)
    a.scatter_rest()
    a.predict()
    b.total = products(3, None)
    cot_other = swap(order(lambda c: c, cotangent), "seq", 1)
    b.scatter_rest()
    b.predict()
    a_steps, b_steps = a.ensemble_steps(), b.ensemble_steps()
    next(a_steps)
    for _ in b.far:
        next(b_steps)
        slope = order(slope_of, pre_act)
        next(a_steps, None)
    cotangents = [
        order(lambda c: jnp.broadcast_to(c[:, None], (steps, 128)), value)
        for value in (cotangent, cot_other)
    ]
    kept = a.early_gradient(cotangents, members, factor)
    a.kept, a.offset = a.gather(kept), 0
    rows_early, rows_late = [blocks[1], blocks[3]], [blocks[0], blocks[2]]
    next(b_steps, None)
    term, kept_back = order(
        lambda g: kept_products(g, hidden, blocks[1], starts), a.kept[0]
    )
    kept = b.early_gradient(cotangents, members, factor)
    a.kept = a.kept[0], order(lambda x: x, a.kept[1])
    a.gradient(cotangents, members, factor, kept)
    b.kept, b.offset = a.rest, steps
    b.gradient(cotangents, members, factor)
    weight_grads, before = order(
        lambda x, y: first_blocks(
            x, y, term, hidden, starts, [1, 3], features, rows_early, kept_back
        ),
        a.share,
        b.share,
    )
    a_other = a.together(1)
    b_other = b.together(1)
    leaving, spread = order(
        lambda x, y, z: leave_to_other(
            (x, blocks[0]), (y, blocks[2]), before, b.sums, z, steps
        ),
        a_other,
        b_other,
        b.other_sums,
    )
    arrived = swap(leaving, "seq", 1)
    weight_grads, before = order(
        lambda x, y, s: last_blocks([x, y], hidden, starts, [0, 2], s, rows_late, before),
        a_other,
        b_other,
        weight_grads,
    )
    act_grads, reward = order(
        lambda g, s: last_grads(g, s, slope, spread, model_width), before, arrived
    )
    return (weight_grads[None], act_grads[:, None, :], reward[0])


def solution(mesh):
    placed = (
        P(("groups", "seq"), "ensemble", "tensor"),
        P("ensemble", "seq", "tensor"),
        P(("groups", "seq")),
    )
    return jax.shard_map(
        body,
        mesh=mesh,
        in_specs=placed,
        out_specs=(
            P(("groups", "ensemble"), "seq", "tensor"),
            P(("groups", "seq"), "ensemble", "tensor"),
            P(("groups", "seq")),
        ),
        check_vma=False,
    )
```
